32 devices in a mesh: layer: 4 (over x, core), row: 2 (over y), col: 4 (over z).
Axes of the slice: x: 2, y: 2, z: 4, core: 2. Of those that a mesh axis runs over, the one named last changes fastest.
Arguments:
- a_blocks: bfloat16 [32, 8, 128, 128], P(('layer', 'row', 'col'))
- a_rows: int32 [32, 8], P(('layer', 'row', 'col')), may hold values from 0 to 15, as said below
- a_count: int32 [32], P(('layer', 'row', 'col')), may hold values from 1 to 8, as said below
- b_panel: bfloat16 [2048, 512], P(('layer', 'row'), 'col'), may hold values from -6 to 6
Outputs:
- flow_out: float32 [2, 2048, 512], P('row', 'layer', 'col')
The draws below stay inside these ranges and needn't reach their ends.
Inputs may be any that keep to these rules, and one draw needn't show every extreme that they name: `a_rows`: within one panel the listed block rows are distinct. `a_count`: some panel's list is full in every draw.
All inputs are finite; a program needn't handle non-finite values.
Results may differ from the reference program's by a relative error of at most 0.0003.
Values may be sent and summed in bfloat16 or wider, within the bound.
No kernel may reach another device: no remote copies, remote signals or barrier semaphores. Data moves between devices by JAX's collectives and lax.ppermute only.
A program may use at most 64 MiB of HBM per device.

```python
import math
import jax
import jax.numpy as jnp
from jax import lax

BS = 128
IB = 16
NA = 8
PANELS = 32
ROWS = 4096
INNER = 2048
COLS = 512
N_ROW = 2
N_COL = 4


def draw_rows(key):
    key = jax.random.fold_in(key, 11)
    panel_keys = jax.random.split(key, PANELS)
    return jax.vmap(lambda subkey: jax.random.permutation(subkey, IB)[:NA])(panel_keys).astype(jnp.int32)


def draw_a_rows(key, part):
    return draw_rows(key)


def draw_a_blocks(key, part):
    row_ids = draw_rows(key)
    key = jax.random.fold_in(key, 3)
    key_scale, key_entries = jax.random.split(key)
    position = jnp.arange(ROWS, dtype=jnp.float32) / (ROWS - 1)
    row_ramp = 2.0 ** position
    entries = jax.random.normal(key_entries, (PANELS, NA, BS, BS), jnp.float32)
    roughness = jnp.exp(jax.random.uniform(key_scale, (ROWS,), jnp.float32, 0.0, 1.15))
    row_scale = row_ramp * roughness / math.sqrt(BS)
    grid_row = jnp.arange(PANELS, dtype=jnp.int32) // N_COL % N_ROW
    global_rows = ((grid_row[:, None] * IB + row_ids)[:, :, None] * BS + jnp.arange(BS, dtype=jnp.int32)).astype(jnp.int32)
    return (entries * row_scale[global_rows][..., None]).astype(jnp.bfloat16)


def draw_a_count(key, part):
    key = jax.random.fold_in(key, 5)
    key_shift, key_full = jax.random.split(key)
    shifts = jax.random.randint(key_shift, (PANELS,), 0, 4)
    counts = jnp.maximum(1, NA // jnp.left_shift(1, shifts))
    full_panel = jax.random.randint(key_full, (), 0, PANELS)
    return counts.at[full_panel].set(NA).astype(jnp.int32)


def shard_levels(stream_key, shape, pieces, least, top_value):
    loudness, own = 1.0, jax.random.fold_in(stream_key, 6)
    for dim, shards_of in pieces:
        heights = jnp.exp(jax.random.uniform(jax.random.fold_in(own, dim), (shards_of,), jnp.float32, least / len(pieces), top_value / len(pieces)))
        loudness = loudness * jnp.repeat(heights, shape[dim] // shards_of).reshape([-1 if axis == dim else 1 for axis in range(len(shape))])
    return loudness


def scatter_about(stream_key, shape, deviation, reach, shards=(), kind=jnp.bfloat16):
    drawn = deviation * jax.random.normal(stream_key, shape, jnp.float32)
    if shards:
        drawn = drawn * shard_levels(stream_key, shape, shards, -0.22, 0.18)
    return jnp.clip(drawn, -reach, reach).astype(kind)


def setup_inputs(seed: int = 0) -> dict:
    streams_of = jax.random.split(jax.random.key(seed), 5)
    return {
        "a_blocks": draw_a_blocks(jax.random.fold_in(streams_of[4], 71), 0),
        "a_rows": draw_a_rows(jax.random.fold_in(streams_of[4], 71), 0),
        "a_count": draw_a_count(jax.random.fold_in(streams_of[4], 71), 0),
        "b_panel": scatter_about(streams_of[3], (INNER, COLS), 1.0, 6.0, ((0, 8), (1, 4))),
    }


def reference(a_blocks, a_rows, a_count, b_panel):
    panels, capacity, block_size, _ = a_blocks.shape
    width = b_panel.shape[1]

    def one_panel(accum, inputs):
        blocks, row_ids, panel_count, panel_id = inputs
        layer_id = panel_id // (N_ROW * N_COL)
        grid_row = (panel_id // N_COL) % N_ROW
        column_id = panel_id % N_COL
        start_row = ((layer_id * N_COL + column_id) * block_size).astype(jnp.int32)
        b_rows = lax.dynamic_slice_in_dim(b_panel, start_row, block_size, 0).astype(jnp.float32)
        products = jnp.einsum('nab,bc->nac', blocks.astype(jnp.float32), b_rows)
        is_valid = (jnp.arange(capacity, dtype=jnp.int32) < panel_count).astype(jnp.float32)
        products = products * is_valid[:, None, None]
        target = (grid_row * IB + row_ids).astype(jnp.int32)
        return accum.at[target].add(products), None

    accum = jnp.zeros((N_ROW * IB, block_size, width), jnp.float32)
    accum, _ = lax.scan(one_panel, accum, (a_blocks, a_rows, a_count, jnp.arange(panels, dtype=jnp.int32)))
    squares = accum * accum
    col_mean = jnp.mean(squares, axis=(0, 1))
    flow_out = squares / (col_mean + 1e-6)
    return flow_out.reshape(N_ROW, IB * block_size, width)
```

```python
import functools

import jax
import jax.numpy as jnp
from jax import lax
from jax.experimental import pallas as pl
from jax.experimental.pallas import tpu as pltpu
from jax.sharding import PartitionSpec as P

IB = 16
CHUNKS = 2
VMEM = pl.BlockSpec(memory_space=pltpu.VMEM)
SMEM = pl.BlockSpec(memory_space=pltpu.SMEM)


def xor_permute(x, axis, mask):
    return lax.ppermute(x, axis, [(i, i ^ mask) for i in range(lax.axis_size(axis))])


def grid_permute(x, layer_mask, row_mask):
    n, m = lax.axis_size("layer"), lax.axis_size("row")
    pairs = [
        (i * m + j, (i ^ layer_mask) * m + (j ^ row_mask)) for i in range(n) for j in range(m)
    ]
    return lax.ppermute(x, ("layer", "row"), pairs)


def partial_kernel(masks, n_layer, place_ref, ids_ref, b_ref, *refs):
    a_refs, (keep_ref, send_ref) = refs[: len(masks)], refs[len(masks) :]
    keep_ref[...] = jnp.zeros_like(keep_ref)
    send_ref[...] = jnp.zeros_like(send_ref)
    layer, col = place_ref[0], place_ref[1]
    per = IB // n_layer
    capacity, rows, depth = a_refs[0].shape
    for mask, a_ref in zip(masks, a_refs, strict=True):
        panel = col ^ mask
        b = b_ref[pl.ds(pl.multiple_of(panel * depth, depth), depth), :]
        a = a_ref[...].reshape(capacity * rows, depth)
        prod = jnp.dot(a, b, preferred_element_type=jnp.float32).reshape(capacity, rows, -1)
        for n in range(capacity):
            block_row = ids_ref[panel, n]
            target = (block_row // per) ^ layer
            slot, sub = target // 2, block_row % per
            is_valid = block_row < IB

            @pl.when(is_valid & (target % 2 == 0))
            def _():
                keep_ref[slot, sub] += prod[n]

            @pl.when(is_valid & (target % 2 == 1))
            def _():
                send_ref[slot, sub] += prod[n]


def square_kernel(n_terms, chunks, *refs):
    ins, (sq_ref, sum_ref) = refs[: n_terms * chunks], refs[n_terms * chunks :]
    total = jnp.zeros(sum_ref.shape, jnp.float32)
    rows = sq_ref.shape[1] // chunks
    for h in range(chunks):
        e = ins[h * n_terms][...]
        for t in range(1, n_terms):
            e = e + ins[h * n_terms + t][...]
        sq = e * e
        sq_ref[:, h * rows : (h + 1) * rows, :] = sq
        total = total + jnp.sum(sq, axis=(0, 1))[None]
    sum_ref[...] = total


def body(a_blocks, a_rows, a_count, b_panel):
    n_layer, n_row, n_col = (lax.axis_size(a) for a in ("layer", "row", "col"))
    _, capacity, block, depth = a_blocks.shape
    width = b_panel.shape[1]
    rows = block // CHUNKS
    a = a_blocks[0]

    parts = [a[:, h * rows : (h + 1) * rows, :] for h in range(CHUNKS)]
    masks = [0]
    held = [[p] for p in parts]
    bit = n_col // 2
    while bit:
        for h in range(CHUNKS):
            held[h] = held[h] + [xor_permute(p, "col", bit) for p in held[h]]
        masks = masks + [m ^ bit for m in masks]
        bit //= 2

    valid = jnp.arange(capacity, dtype=jnp.int32)[None, :] < a_count[:, None]
    ids = lax.all_gather(jnp.where(valid, a_rows, IB), "col", axis=0, tiled=True)
    b_rows = lax.all_gather(b_panel, "row", axis=0, tiled=True)
    place = jnp.stack([lax.axis_index("layer"), lax.axis_index("col")]).astype(jnp.int32)

    per = IB // n_layer
    half = jax.ShapeDtypeStruct((n_layer // 2, per, rows, width), jnp.float32)
    terms = []
    for h in range(CHUNKS):
        keep, send = pl.pallas_call(
            functools.partial(partial_kernel, masks, n_layer),
            out_shape=(half, half),
            in_specs=[SMEM, SMEM] + [VMEM] * (1 + len(masks)),
            out_specs=(VMEM, VMEM),
            name="partial_rows",
        )(place, ids, b_rows, *held[h])
        got = xor_permute(send, "layer", 1)
        mine = [keep[0], got[0]]
        others = [keep[k] + got[k] for k in range(1, n_layer // 2)]
        bit = n_layer // 2
        n_slots = n_layer // 2
        slots = {k: others[k - 1] for k in range(1, n_slots)}
        step = n_slots // 2
        while step:
            got = {k: xor_permute(slots[k], "layer", 2 * step) for k in range(step, 2 * step)}
            mine.append(got[step])
            slots = {k: slots[k] + got[k + step] for k in range(1, step)}
            step //= 2
        terms += mine
    n_terms = len(terms) // CHUNKS

    sq, col_sum = pl.pallas_call(
        functools.partial(square_kernel, n_terms, CHUNKS),
        out_shape=(
            jax.ShapeDtypeStruct((per, block, width), jnp.float32),
            jax.ShapeDtypeStruct((1, width), jnp.float32),
        ),
        in_specs=[VMEM] * len(terms),
        out_specs=(VMEM, VMEM),
        name="squares",
    )(*terms)

    col_sum = col_sum + xor_permute(col_sum, "layer", 1)
    others = [
        grid_permute(col_sum, i, j)
        for i in range(0, n_layer, 2)
        for j in range(n_row)
        if i or j
    ]
    for other in others:
        col_sum = col_sum + other
    scale = 1.0 / (col_sum * (1.0 / (n_row * IB * block)) + 1e-06)
    return (sq * scale).reshape(1, per * block, width)


def solution(mesh):
    return jax.shard_map(
        body,
        mesh=mesh,
        in_specs=(
            P(("layer", "row", "col"), None, None, None),
            P(("layer", "row", "col"), None),
            P(("layer", "row", "col")),
            P(("layer", "row"), "col"),
        ),
        out_specs=P("row", "layer", "col"),
        check_vma=False,
    )
```

```python
import functools

import jax
import jax.numpy as jnp
from jax import lax
from jax.experimental import pallas as pl
from jax.experimental.pallas import tpu as pltpu
from jax.sharding import PartitionSpec as P

IB = 16
CUTS = (32, 96)
PAD = 16
VMEM = pl.BlockSpec(memory_space=pltpu.VMEM)
SMEM = pl.BlockSpec(memory_space=pltpu.SMEM)


def pin(x):
    return pltpu.with_memory_space_constraint(x, pltpu.VMEM)


def xor_permute(x, axis, mask):
    return lax.ppermute(x, axis, [(i, i ^ mask) for i in range(lax.axis_size(axis))])


def grid_permute(x, layer_mask, row_mask):
    n, m = lax.axis_size("layer"), lax.axis_size("row")
    pairs = [
        (i * m + j, (i ^ layer_mask) * m + (j ^ row_mask)) for i in range(n) for j in range(m)
    ]
    return lax.ppermute(x, ("layer", "row"), pairs)


def product_kernel(masks, n_layer, n_row, capacity, rows, depth, ids_ref, *refs):
    n_slots, n_held = n_layer // 2, 2 * len(masks)
    b_refs, a_refs = refs[:2], refs[2 : 2 + n_held]
    out_refs = refs[2 + n_held : 2 + n_held + n_slots]
    where_ref, lhs_ref = refs[2 + n_held + n_slots :]
    layer, row, col = (lax.axis_index(n) for n in ("layer", "row", "col"))
    per, per_row = IB // n_layer, len(masks) // n_row
    for k in range(n_held):
        for i in range(IB + 1):
            where_ref[k, i] = -1
        for n in range(capacity):
            where_ref[k, ids_ref[k, n]] = n
    rhs = []
    for k in range(n_held):
        panel = col ^ masks[k // 2]
        start = (((panel // per_row) ^ row) * per_row + panel % per_row) * depth
        rhs.append(b_refs[k % 2][pl.ds(pl.multiple_of(start, depth), depth), :])
    rhs = jnp.concatenate(rhs, axis=0)
    for slot in range(n_slots):
        for sub in range(per):
            block_row = (layer ^ (2 * slot)) * per + sub
            for k in range(n_held):
                n = where_ref[k, block_row]
                start = pl.multiple_of(jnp.maximum(n, 0) * rows, rows)
                a = a_refs[k][pl.ds(start, rows), :]
                lhs_ref[sub * rows : (sub + 1) * rows, k * depth : (k + 1) * depth] = jnp.where(
                    n >= 0, a, jnp.zeros_like(a)
                )
        out_refs[slot][...] = jnp.dot(
            lhs_ref[...], rhs, preferred_element_type=jnp.float32
        ).reshape(out_refs[slot].shape)


def body(a_blocks, a_rows, a_count, b_panel):
    n_layer, n_row, n_col = (lax.axis_size(a) for a in ("layer", "row", "col"))
    _, capacity, block, depth = a_blocks.shape
    width = b_panel.shape[1]
    a = a_blocks[0]

    valid = jnp.arange(capacity, dtype=jnp.int32)[None, :] < a_count[:, None]
    own_ids = jnp.where(valid, a_rows, IB).astype(a.dtype)
    own_ids = jnp.pad(own_ids, ((0, PAD - 1), (0, depth - capacity)))
    parts, start = [], 0
    for h, rows in enumerate(CUTS):
        part = a[:, start : start + rows, :].reshape(capacity * rows, depth)
        parts.append(part if h else jnp.concatenate([part, own_ids]))
        start += rows

    masks = [0]
    held = [[p] for p in parts]
    bit = n_col // 2
    while bit:
        for h in range(len(CUTS)):
            held[h] = held[h] + [xor_permute(p, "col", bit) for p in held[h]]
        masks = masks + [m ^ bit for m in masks]
        bit //= 2

    b_rows = [b_panel]
    bit = 1
    while bit < n_row:
        b_rows = b_rows + [xor_permute(b, "row", bit) for b in b_rows]
        bit *= 2
    b_rows = jnp.concatenate(b_rows)
    b_other = xor_permute(b_rows, "layer", 1)

    pairs = [[q for p in held[h] for q in (p, xor_permute(p, "layer", 1))] for h in range(len(CUTS))]
    ids = jnp.stack([p[capacity * CUTS[0], :capacity] for p in pairs[0]]).astype(jnp.int32)

    per, n_slots = IB // n_layer, n_layer // 2
    terms = []
    for h, rows in enumerate(CUTS):
        slots = pl.pallas_call(
            functools.partial(
                product_kernel, masks, n_layer, n_row, capacity, rows, depth
            ),
            out_shape=[pltpu.VMEM((per, rows, width), jnp.float32)] * n_slots,
            in_specs=[SMEM] + [VMEM] * (2 + len(pairs[h])),
            out_specs=[VMEM] * n_slots,
            scratch_shapes=[
                pltpu.SMEM((len(pairs[h]), IB + 1), jnp.int32),
                pltpu.VMEM((per * rows, len(pairs[h]) * depth), jnp.bfloat16),
            ],
            name="partial_rows",
        )(ids, *(pin(x) for x in (b_rows, b_other, *pairs[h])))
        step = n_slots // 2
        mine = [slots[0]]
        while step:
            got = [xor_permute(s, "layer", 2 * step) for s in slots[step : 2 * step]]
            mine.append(got[0])
            slots = [None] + [s + g for s, g in zip(slots[1:step], got[1:])]
            step //= 2
        terms += mine
    n_terms = len(terms) // len(CUTS)

    expanded = [sum(terms[h * n_terms : (h + 1) * n_terms]) for h in range(len(CUTS))]
    sq = jnp.concatenate([e * e for e in expanded], axis=1)
    col_sum = jnp.sum(sq, axis=(0, 1))[None]

    col_sum = col_sum + xor_permute(col_sum, "layer", 1)
    others = [
        grid_permute(col_sum, i, j)
        for i in range(0, n_layer, 2)
        for j in range(n_row)
        if i or j
    ]
    for other in others:
        col_sum = col_sum + other
    scale = 1.0 / (col_sum * (1.0 / (n_row * IB * block)) + 1e-06)
    return (sq * scale).reshape(1, per * block, width)


def solution(mesh):
    return jax.shard_map(
        body,
        mesh=mesh,
        in_specs=(
            P(("layer", "row", "col"), None, None, None),
            P(("layer", "row", "col"), None),
            P(("layer", "row", "col")),
            P(("layer", "row"), "col"),
        ),
        out_specs=P("row", "layer", "col"),
        check_vma=False,
    )
```

```python
import functools

import jax
import jax.numpy as jnp
from jax import lax
from jax.experimental import pallas as pl
from jax.experimental.pallas import tpu as pltpu
from jax.sharding import PartitionSpec as P

IB = 16
VMEM = pl.BlockSpec(memory_space=pltpu.VMEM)
SMEM = pl.BlockSpec(memory_space=pltpu.SMEM)


def pin(x):
    return pltpu.with_memory_space_constraint(x, pltpu.VMEM)


def xor_permute(x, axis, mask):
    return lax.ppermute(x, axis, [(i, i ^ mask) for i in range(lax.axis_size(axis))])


def grid_permute(x, layer_mask, row_mask, col_mask):
    n, m, c = (lax.axis_size(a) for a in ("layer", "row", "col"))
    pairs = [
        ((i * m + j) * c + k, ((i ^ layer_mask) * m + (j ^ row_mask)) * c + (k ^ col_mask))
        for i in range(n)
        for j in range(m)
        for k in range(c)
    ]
    return lax.ppermute(x, ("layer", "row", "col"), pairs)


def product_kernel(masks, n_layer, n_row, n_col, ids_ref, *refs):
    n_slots, n_held = n_layer // 2, 2 * len(masks)
    b_refs, a_refs = refs[:4], refs[4 : 4 + n_held]
    out_refs = refs[4 + n_held : -2]
    where_ref, lhs_ref = refs[-2:]
    layer, row, col = (lax.axis_index(n) for n in ("layer", "row", "col"))
    per, per_row = IB // n_layer, n_col // n_row // 2
    capacity, block, depth = a_refs[0].shape
    rhs = []
    for k in range(n_held):
        other, place = k % 2, k // 2
        for i in range(IB + 1):
            where_ref[k, i] = -1
        for n in range(capacity):
            where_ref[k, ids_ref[k, n]] = n
        pair = (col ^ masks[place]) // 2
        start = (((pair // per_row) ^ row) * per_row + pair % per_row) * depth
        at = pl.ds(pl.multiple_of(start, depth), depth)
        rhs.append(jnp.concatenate([b_refs[2 * m + other][at, :] for m in range(2)], axis=1))
    rhs = jnp.concatenate(rhs, axis=0)
    width = rhs.shape[1] // 2
    for slot in range(n_slots):
        for sub in range(per):
            block_row = (layer ^ (2 * slot)) * per + sub
            for k in range(n_held):
                n = where_ref[k, block_row]
                a = a_refs[k][jnp.maximum(n, 0)]
                lhs_ref[slot, sub * block : (sub + 1) * block, k * depth : (k + 1) * depth] = (
                    jnp.where(n >= 0, a, jnp.zeros_like(a))
                )
        out = jnp.dot(lhs_ref[slot], rhs, preferred_element_type=jnp.float32)
        for m in range(2):
            out_refs[2 * slot + m][...] = out[:, m * width : (m + 1) * width]


def products(masks, ids, b_refs, panels):
    n_layer, n_row, n_col = (lax.axis_size(a) for a in ("layer", "row", "col"))
    _, block, depth = panels[0].shape
    rows, n_slots, width = IB // n_layer * block, n_layer // 2, b_refs[0].shape[1]
    ins = [*b_refs, *panels]
    return pl.pallas_call(
        functools.partial(product_kernel, masks, n_layer, n_row, n_col),
        out_shape=[pltpu.VMEM((rows, width), jnp.float32)] * (2 * n_slots),
        in_specs=[SMEM] + [VMEM] * len(ins),
        out_specs=[VMEM] * (2 * n_slots),
        scratch_shapes=[
            pltpu.SMEM((len(panels), IB + 1), jnp.int32),
            pltpu.VMEM((n_slots, rows, len(panels) * depth), jnp.bfloat16),
        ],
        name="partial_rows",
    )(ids, *(pin(x) for x in ins))


def body(a_blocks, a_rows, a_count, b_panel):
    n_layer, n_row, n_col = (lax.axis_size(a) for a in ("layer", "row", "col"))
    _, capacity, block, _ = a_blocks.shape

    def other(x):
        return xor_permute(x, "layer", 1)

    masks, panels = [0], [a_blocks[0]]
    valid = jnp.arange(capacity, dtype=jnp.int32)[None, :] < a_count[:, None]
    ids = jnp.where(valid, a_rows, IB)
    ids = jnp.concatenate([ids, other(ids)])
    bit = n_col // 2
    while bit > 1:
        panels = panels + [xor_permute(p, "col", bit) for p in panels]
        ids = jnp.concatenate([ids, xor_permute(ids, "col", bit)])
        masks = masks + [m ^ bit for m in masks]
        bit //= 2

    b_rows = [b_panel]
    bit = 1
    while bit < n_row:
        b_rows = b_rows + [xor_permute(b, "row", bit) for b in b_rows]
        bit *= 2
    b_rows = jnp.concatenate(b_rows).reshape(-1, 2, *b_panel.shape[-1:] * 2)
    parity = lax.axis_index("col") % 2
    b_mine, b_near = (
        lax.dynamic_index_in_dim(b_rows, p, 1, False).reshape(-1, b_panel.shape[1])
        for p in (parity, 1 - parity)
    )
    b_refs = [b_mine, other(b_mine), xor_permute(b_near, "col", 1)]

    far, ids, b_refs = lax.optimization_barrier((panels[1:], ids, b_refs))
    panels[1:] = far
    b_refs.append(other(b_refs[2]))
    panels = [x for p in panels for x in (p, other(p))]
    parts = products(masks, ids, b_refs, panels)

    expanded = parts[0]
    for k in range(1, n_layer):
        expanded = expanded + grid_permute(parts[k], 2 * (k // 2), 0, k % 2)
    sq = expanded * expanded
    col_sum = jnp.sum(sq, axis=0)[None]

    col_sum = col_sum + xor_permute(col_sum, "layer", 1)
    others = [
        grid_permute(col_sum, i, j, 0)
        for i in range(0, n_layer, 2)
        for j in range(n_row)
        if i or j
    ]
    for other in others:
        col_sum = col_sum + other
    scale = 1.0 / (col_sum * (1.0 / (n_row * IB * block)) + 1e-06)
    return (sq * scale)[None]


def solution(mesh):
    return jax.shard_map(
        body,
        mesh=mesh,
        in_specs=(
            P(("layer", "row", "col"), None, None, None),
            P(("layer", "row", "col"), None),
            P(("layer", "row", "col")),
            P(("layer", "row"), "col"),
        ),
        out_specs=P("row", "layer", "col"),
        check_vma=False,
    )
```

```python
import functools

import jax
import jax.numpy as jnp
from jax import lax
from jax.experimental import pallas as pl
from jax.experimental.pallas import tpu as pltpu
from jax.sharding import PartitionSpec as P

IB = 16
BITS = 24
VMEM = pl.BlockSpec(memory_space=pltpu.VMEM)
SMEM = pl.BlockSpec(memory_space=pltpu.SMEM)


def pin(x):
    return pltpu.with_memory_space_constraint(x, pltpu.VMEM)


def xor_permute(x, axis, mask):
    return lax.ppermute(x, axis, [(i, i ^ mask) for i in range(lax.axis_size(axis))])


def grid_permute(x, layer_mask, row_mask, col_mask):
    n, m, c = (lax.axis_size(a) for a in ("layer", "row", "col"))
    pairs = [
        ((i * m + j) * c + k, ((i ^ layer_mask) * m + (j ^ row_mask)) * c + (k ^ col_mask))
        for i in range(n)
        for j in range(m)
        for k in range(c)
    ]
    return lax.ppermute(x, ("layer", "row", "col"), pairs)


def power_of_two(k):
    scale = jnp.ones(k.shape, jnp.float32)
    for b in range(7):
        factor = jnp.where(k < 0, 2.0 ** -(2**b), 2.0 ** (2**b))
        scale = jnp.where((jnp.abs(k) >> b) & 1 == 1, scale * factor, scale)
    return scale


def pack(part, out_ref):
    top = jnp.max(jnp.abs(part), axis=0, keepdims=True)
    k = jnp.clip(jnp.ceil(jnp.log2(top)), -100.0, 125.0).astype(jnp.int32) + 1
    q = jnp.floor(part * power_of_two(BITS - 1 - k) + 0.5).astype(jnp.int32)
    rows = part.shape[0] // 4
    a, b, c, d = (q[i * rows : (i + 1) * rows] for i in range(4))
    out_ref[:rows] = (a << 8) | (d & 255)
    out_ref[rows : 2 * rows] = (b << 8) | ((d >> 8) & 255)
    out_ref[2 * rows : 3 * rows] = (c << 8) | ((d >> 16) & 255)
    out_ref[3 * rows :] = jnp.broadcast_to(k, (8, part.shape[1]))


def square_kernel(mine_ref, *refs):
    coded_refs, (sq_ref, sum_ref) = refs[:-2], refs[-2:]
    rows = mine_ref.shape[0] // 4
    scales = [power_of_two(ref[3 * rows : 3 * rows + 1] - (BITS - 1)) for ref in coded_refs]
    total = jnp.zeros(sum_ref.shape, jnp.float32)
    for i in range(4):
        at = slice(i * rows, (i + 1) * rows)
        e = mine_ref[at]
        for ref, scale in zip(coded_refs, scales):
            if i < 3:
                q = ref[at] >> 8
            else:
                w = [ref[j * rows : (j + 1) * rows] for j in range(3)]
                q = (w[0] & 255) | ((w[1] & 255) << 8) | ((w[2] << 24) >> 8)
            e = e + q.astype(jnp.float32) * scale
        sq = e * e
        sq_ref[at] = sq
        total = total + jnp.sum(sq, axis=0, keepdims=True)
    sum_ref[...] = total


def product_kernel(masks, n_layer, n_row, n_col, ids_ref, *refs):
    n_slots, n_held = n_layer // 2, 2 * len(masks)
    b_refs, a_refs = refs[:4], refs[4 : 4 + n_held]
    out_refs = refs[4 + n_held : -2]
    where_ref, lhs_ref = refs[-2:]
    layer, row, col = (lax.axis_index(n) for n in ("layer", "row", "col"))
    per, per_row = IB // n_layer, n_col // n_row // 2
    capacity, block, depth = a_refs[0].shape
    rhs = []
    for k in range(n_held):
        other, place = k % 2, k // 2
        for i in range(IB + 1):
            where_ref[k, i] = -1
        for n in range(capacity):
            where_ref[k, ids_ref[k, n]] = n
        pair = (col ^ masks[place]) // 2
        start = (((pair // per_row) ^ row) * per_row + pair % per_row) * depth
        at = pl.ds(pl.multiple_of(start, depth), depth)
        rhs.append(jnp.concatenate([b_refs[2 * m + other][at, :] for m in range(2)], axis=1))
    rhs = jnp.concatenate(rhs, axis=0)
    width = rhs.shape[1] // 2
    for slot in range(n_slots):
        for sub in range(per):
            block_row = (layer ^ (2 * slot)) * per + sub
            for k in range(n_held):
                n = where_ref[k, block_row]
                a = a_refs[k][jnp.maximum(n, 0)]
                lhs_ref[slot, sub * block : (sub + 1) * block, k * depth : (k + 1) * depth] = (
                    jnp.where(n >= 0, a, jnp.zeros_like(a))
                )
        out = jnp.dot(lhs_ref[slot], rhs, preferred_element_type=jnp.float32)
        for m in range(2):
            part, out_ref = out[:, m * width : (m + 1) * width], out_refs[2 * slot + m]
            if slot or m:
                pack(part, out_ref)
            else:
                out_ref[...] = part


def products(masks, ids, b_refs, panels):
    n_layer, n_row, n_col = (lax.axis_size(a) for a in ("layer", "row", "col"))
    _, block, depth = panels[0].shape
    rows, n_slots, width = IB // n_layer * block, n_layer // 2, b_refs[0].shape[1]
    ins = [*b_refs, *panels]
    return pl.pallas_call(
        functools.partial(product_kernel, masks, n_layer, n_row, n_col),
        out_shape=[pltpu.VMEM((rows, width), jnp.float32)]
        + [pltpu.VMEM((rows // 4 * 3 + 8, width), jnp.int32)] * (2 * n_slots - 1),
        in_specs=[SMEM] + [VMEM] * len(ins),
        out_specs=[VMEM] * (2 * n_slots),
        scratch_shapes=[
            pltpu.SMEM((len(panels), IB + 1), jnp.int32),
            pltpu.VMEM((n_slots, rows, len(panels) * depth), jnp.bfloat16),
        ],
        name="partial_rows",
    )(ids, *(pin(x) for x in ins))


def body(a_blocks, a_rows, a_count, b_panel):
    n_layer, n_row, n_col = (lax.axis_size(a) for a in ("layer", "row", "col"))
    _, capacity, block, _ = a_blocks.shape

    def other(x):
        return xor_permute(x, "layer", 1)

    masks, panels = [0], [a_blocks[0]]
    valid = jnp.arange(capacity, dtype=jnp.int32)[None, :] < a_count[:, None]
    ids = jnp.where(valid, a_rows, IB)
    ids = jnp.concatenate([ids, other(ids)])
    bit = n_col // 2
    while bit > 1:
        panels = panels + [xor_permute(p, "col", bit) for p in panels]
        ids = jnp.concatenate([ids, xor_permute(ids, "col", bit)])
        masks = masks + [m ^ bit for m in masks]
        bit //= 2

    b_rows = [b_panel]
    bit = 1
    while bit < n_row:
        b_rows = b_rows + [xor_permute(b, "row", bit) for b in b_rows]
        bit *= 2
    b_rows = jnp.concatenate(b_rows).reshape(-1, 2, *b_panel.shape[-1:] * 2)
    parity = lax.axis_index("col") % 2
    b_mine, b_near = (
        lax.dynamic_index_in_dim(b_rows, p, 1, False).reshape(-1, b_panel.shape[1])
        for p in (parity, 1 - parity)
    )
    b_refs = [b_mine, other(b_mine), xor_permute(b_near, "col", 1)]

    far, ids, b_refs = lax.optimization_barrier((panels[1:], ids, b_refs))
    panels[1:] = far
    b_refs.append(other(b_refs[2]))
    panels = [x for p in panels for x in (p, other(p))]
    parts = products(masks, ids, b_refs, panels)

    parts = [parts[0]] + [grid_permute(parts[k], 2 * (k // 2), 0, k % 2) for k in range(1, n_layer)]
    sq, col_sum = pl.pallas_call(
        square_kernel,
        out_shape=(
            pltpu.VMEM(parts[0].shape, jnp.float32),
            pltpu.VMEM((1, parts[0].shape[1]), jnp.float32),
        ),
        in_specs=[VMEM] * len(parts),
        out_specs=(VMEM, VMEM),
        name="squares",
    )(*(pin(x) for x in parts))

    col_sum = col_sum + xor_permute(col_sum, "layer", 1)
    others = [
        grid_permute(col_sum, i, j, 0)
        for i in range(0, n_layer, 2)
        for j in range(n_row)
        if i or j
    ]
    for other in others:
        col_sum = col_sum + other
    scale = 1.0 / (col_sum * (1.0 / (n_row * IB * block)) + 1e-06)
    return (sq * scale)[None]


def solution(mesh):
    return jax.shard_map(
        body,
        mesh=mesh,
        in_specs=(
            P(("layer", "row", "col"), None, None, None),
            P(("layer", "row", "col"), None),
            P(("layer", "row", "col")),
            P(("layer", "row"), "col"),
        ),
        out_specs=P("row", "layer", "col"),
        check_vma=False,
    )
```

```python
import functools

import jax
import jax.numpy as jnp
from jax import lax
from jax.experimental import pallas as pl
from jax.experimental.pallas import tpu as pltpu
from jax.sharding import PartitionSpec as P

IB = 16
BITS = 20
VMEM = pl.BlockSpec(memory_space=pltpu.VMEM)
SMEM = pl.BlockSpec(memory_space=pltpu.SMEM)


def pin(x):
    return pltpu.with_memory_space_constraint(x, pltpu.VMEM)


def xor_permute(x, axis, mask):
    return lax.ppermute(x, axis, [(i, i ^ mask) for i in range(lax.axis_size(axis))])


def grid_permute(x, layer_mask, row_mask, col_mask):
    n, m, c = (lax.axis_size(a) for a in ("layer", "row", "col"))
    pairs = [
        ((i * m + j) * c + k, ((i ^ layer_mask) * m + (j ^ row_mask)) * c + (k ^ col_mask))
        for i in range(n)
        for j in range(m)
        for k in range(c)
    ]
    return lax.ppermute(x, ("layer", "row", "col"), pairs)


def power_of_two(k):
    scale = jnp.ones(k.shape, jnp.float32)
    for b in range(7):
        factor = jnp.where(k < 0, 2.0 ** -(2**b), 2.0 ** (2**b))
        scale = jnp.where((jnp.abs(k) >> b) & 1 == 1, scale * factor, scale)
    return scale


def pack(part, out_ref):
    top = jnp.max(jnp.abs(part), axis=0, keepdims=True)
    k = jnp.clip(jnp.ceil(jnp.log2(top) + 0.01), -100.0, 126.0).astype(jnp.int32)
    q = jnp.floor(part * power_of_two(BITS - 1 - k) + 0.5).astype(jnp.int32)
    rows = part.shape[0] // 8
    q = [q[i * rows : (i + 1) * rows] for i in range(8)]
    low = [
        q[5] & 4095,
        ((q[5] >> 12) & 255) | ((q[6] & 15) << 8),
        (q[6] >> 4) & 4095,
        ((q[6] >> 16) & 15) | ((q[7] & 255) << 4),
        (q[7] >> 8) & 4095,
    ]
    for i in range(5):
        out_ref[i * rows : (i + 1) * rows] = (q[i] << 12) | low[i]
    out_ref[5 * rows :] = jnp.broadcast_to(k, (8, part.shape[1]))


def unpack(ref, rows, i):
    w = [ref[j * rows : (j + 1) * rows] for j in ([i] if i < 5 else range(5))]
    if i < 5:
        return w[0] >> 12
    if i == 5:
        return (w[0] & 4095) | ((w[1] << 24) >> 12)
    if i == 6:
        return ((w[1] >> 8) & 15) | ((w[2] & 4095) << 4) | ((w[3] << 28) >> 12)
    return ((w[3] >> 4) & 255) | ((w[4] << 20) >> 12)


def square_kernel(mine_ref, *refs):
    coded_refs, (sq_ref, sum_ref) = refs[:-2], refs[-2:]
    rows = mine_ref.shape[0] // 8
    scales = [power_of_two(ref[5 * rows : 5 * rows + 1] - (BITS - 1)) for ref in coded_refs]
    total = jnp.zeros(sum_ref.shape, jnp.float32)
    for i in range(8):
        at = slice(i * rows, (i + 1) * rows)
        e = mine_ref[at]
        for ref, scale in zip(coded_refs, scales):
            e = e + unpack(ref, rows, i).astype(jnp.float32) * scale
        sq = e * e
        sq_ref[at] = sq
        total = total + jnp.sum(sq, axis=0, keepdims=True)
    sum_ref[...] = total


def product_kernel(masks, n_layer, n_row, n_col, ids_ref, *refs):
    n_slots, n_held = n_layer // 2, 2 * len(masks)
    b_refs, a_refs = refs[:4], refs[4 : 4 + n_held]
    out_refs = refs[4 + n_held : -2]
    where_ref, lhs_ref = refs[-2:]
    layer, row, col = (lax.axis_index(n) for n in ("layer", "row", "col"))
    per, per_row = IB // n_layer, n_col // n_row // 2
    capacity, block, depth = a_refs[0].shape
    rhs = []
    for k in range(n_held):
        other, place = k % 2, k // 2
        for i in range(IB + 1):
            where_ref[k, i] = -1
        for n in range(capacity):
            where_ref[k, ids_ref[k, n]] = n
        pair = (col ^ masks[place]) // 2
        start = (((pair // per_row) ^ row) * per_row + pair % per_row) * depth
        at = pl.ds(pl.multiple_of(start, depth), depth)
        rhs.append(jnp.concatenate([b_refs[2 * m + other][at, :] for m in range(2)], axis=1))
    rhs = jnp.concatenate(rhs, axis=0)
    width = rhs.shape[1] // 2
    for slot in range(n_slots):
        for sub in range(per):
            block_row = (layer ^ (2 * slot)) * per + sub
            for k in range(n_held):
                n = where_ref[k, block_row]
                a = a_refs[k][jnp.maximum(n, 0)]
                lhs_ref[slot, sub * block : (sub + 1) * block, k * depth : (k + 1) * depth] = (
                    jnp.where(n >= 0, a, jnp.zeros_like(a))
                )
        out = jnp.dot(lhs_ref[slot], rhs, preferred_element_type=jnp.float32)
        for m in range(2):
            part, out_ref = out[:, m * width : (m + 1) * width], out_refs[2 * slot + m]
            if slot or m:
                pack(part, out_ref)
            else:
                out_ref[...] = part


def products(masks, ids, b_refs, panels):
    n_layer, n_row, n_col = (lax.axis_size(a) for a in ("layer", "row", "col"))
    _, block, depth = panels[0].shape
    rows, n_slots, width = IB // n_layer * block, n_layer // 2, b_refs[0].shape[1]
    ins = [*b_refs, *panels]
    return pl.pallas_call(
        functools.partial(product_kernel, masks, n_layer, n_row, n_col),
        out_shape=[pltpu.VMEM((rows, width), jnp.float32)]
        + [pltpu.VMEM((rows // 8 * 5 + 8, width), jnp.int32)] * (2 * n_slots - 1),
        in_specs=[SMEM] + [VMEM] * len(ins),
        out_specs=[VMEM] * (2 * n_slots),
        scratch_shapes=[
            pltpu.SMEM((len(panels), IB + 1), jnp.int32),
            pltpu.VMEM((n_slots, rows, len(panels) * depth), jnp.bfloat16),
        ],
        name="partial_rows",
    )(ids, *(pin(x) for x in ins))


def body(a_blocks, a_rows, a_count, b_panel):
    n_layer, n_row, n_col = (lax.axis_size(a) for a in ("layer", "row", "col"))
    _, capacity, block, _ = a_blocks.shape

    def other(x):
        return xor_permute(x, "layer", 1)

    masks, panels = [0], [a_blocks[0]]
    valid = jnp.arange(capacity, dtype=jnp.int32)[None, :] < a_count[:, None]
    ids = jnp.where(valid, a_rows, IB)
    ids = jnp.concatenate([ids, other(ids)])
    bit = n_col // 2
    while bit > 1:
        panels = panels + [xor_permute(p, "col", bit) for p in panels]
        ids = jnp.concatenate([ids, xor_permute(ids, "col", bit)])
        masks = masks + [m ^ bit for m in masks]
        bit //= 2

    b_rows = [b_panel]
    bit = 1
    while bit < n_row:
        b_rows = b_rows + [xor_permute(b, "row", bit) for b in b_rows]
        bit *= 2
    b_rows = jnp.concatenate(b_rows).reshape(-1, 2, *b_panel.shape[-1:] * 2)
    parity = lax.axis_index("col") % 2
    b_mine, b_near = (
        lax.dynamic_index_in_dim(b_rows, p, 1, False).reshape(-1, b_panel.shape[1])
        for p in (parity, 1 - parity)
    )
    b_refs = [b_mine, other(b_mine), xor_permute(b_near, "col", 1)]

    far, ids, b_refs = lax.optimization_barrier((panels[1:], ids, b_refs))
    panels[1:] = far
    b_refs.append(other(b_refs[2]))
    panels = [x for p in panels for x in (p, other(p))]
    parts = products(masks, ids, b_refs, panels)

    parts = [parts[0]] + [grid_permute(parts[k], 2 * (k // 2), 0, k % 2) for k in range(1, n_layer)]
    sq, col_sum = pl.pallas_call(
        square_kernel,
        out_shape=(
            pltpu.VMEM(parts[0].shape, jnp.float32),
            pltpu.VMEM((1, parts[0].shape[1]), jnp.float32),
        ),
        in_specs=[VMEM] * len(parts),
        out_specs=(VMEM, VMEM),
        name="squares",
    )(*(pin(x) for x in parts))

    col_sum = col_sum + xor_permute(col_sum, "layer", 1)
    others = [
        grid_permute(col_sum, i, j, 0)
        for i in range(0, n_layer, 2)
        for j in range(n_row)
        if i or j
    ]
    for other in others:
        col_sum = col_sum + other
    scale = 1.0 / (col_sum * (1.0 / (n_row * IB * block)) + 1e-06)
    return (sq * scale)[None]


def solution(mesh):
    return jax.shard_map(
        body,
        mesh=mesh,
        in_specs=(
            P(("layer", "row", "col"), None, None, None),
            P(("layer", "row", "col"), None),
            P(("layer", "row", "col")),
            P(("layer", "row"), "col"),
        ),
        out_specs=P("row", "layer", "col"),
        check_vma=False,
    )
```

```python
import functools

import jax
import jax.numpy as jnp
import numpy as np
from jax import lax
from jax.experimental import pallas as pl
from jax.experimental.pallas import tpu as pltpu
from jax.sharding import PartitionSpec as P

IB = 16
AXES = ("layer", "row", "col")
BITS = 20
VMEM = pl.BlockSpec(memory_space=pltpu.VMEM)
SMEM = pl.BlockSpec(memory_space=pltpu.SMEM)


def pin(x):
    return pltpu.with_memory_space_constraint(x, pltpu.VMEM)


def xor_permute(x, axis, mask):
    return lax.ppermute(x, axis, [(i, i ^ mask) for i in range(lax.axis_size(axis))])


def grid_permute(x, masks, other_masks=None):
    sizes = [lax.axis_size(a) for a in AXES]
    pairs = []
    for source, at in enumerate(np.ndindex(*sizes)):
        by = other_masks if other_masks and at[0] % 2 else masks
        target = [i ^ m for i, m in zip(at, by, strict=True)]
        pairs.append((source, int(np.ravel_multi_index(target, sizes))))
    return lax.ppermute(x, AXES, pairs)


def sum_over_devices(x):
    n_layer, n_row, _ = (lax.axis_size(a) for a in AXES)
    chips = [(i, j, 0) for i in range(0, n_layer, 2) for j in range(n_row)][:0:-1]
    got = [grid_permute(x, chips.pop(0))] if len(chips) % 2 else []
    x = x + xor_permute(x, "layer", 1)
    got += [grid_permute(x, *chips[k : k + 2]) for k in range(0, len(chips), 2)]
    got = sum(got)
    return x + (got + xor_permute(got, "layer", 1))


def power_of_two(k):
    scale = jnp.ones(k.shape, jnp.float32)
    for b in range(7):
        factor = jnp.where(k < 0, 2.0 ** -(2**b), 2.0 ** (2**b))
        scale = jnp.where((jnp.abs(k) >> b) & 1 == 1, scale * factor, scale)
    return scale


def pack(part, out_ref):
    top = jnp.max(jnp.abs(part), axis=0, keepdims=True)
    k = jnp.clip(jnp.ceil(jnp.log2(top) + 0.01), -100.0, 126.0).astype(jnp.int32)
    q = jnp.floor(part * power_of_two(BITS - 1 - k) + 0.5).astype(jnp.int32)
    rows = part.shape[0] // 8
    q = [q[i * rows : (i + 1) * rows] for i in range(8)]
    low = [
        q[5] & 4095,
        ((q[5] >> 12) & 255) | ((q[6] & 15) << 8),
        (q[6] >> 4) & 4095,
        ((q[6] >> 16) & 15) | ((q[7] & 255) << 4),
        (q[7] >> 8) & 4095,
    ]
    for i in range(5):
        out_ref[i * rows : (i + 1) * rows] = (q[i] << 12) | low[i]
    out_ref[5 * rows :] = jnp.broadcast_to(k, (8, part.shape[1]))


def unpack(ref, rows, i):
    w = [ref[j * rows : (j + 1) * rows] for j in ([i] if i < 5 else range(5))]
    if i < 5:
        return w[0] >> 12
    if i == 5:
        return (w[0] & 4095) | ((w[1] << 24) >> 12)
    if i == 6:
        return ((w[1] >> 8) & 15) | ((w[2] & 4095) << 4) | ((w[3] << 28) >> 12)
    return ((w[3] >> 4) & 255) | ((w[4] << 20) >> 12)


def square_kernel(mine_ref, *refs):
    coded_refs, (sq_ref, sum_ref) = refs[:-2], refs[-2:]
    rows = mine_ref.shape[0] // 8
    scales = [power_of_two(ref[5 * rows : 5 * rows + 1] - (BITS - 1)) for ref in coded_refs]
    total = jnp.zeros(sum_ref.shape, jnp.float32)
    for i in range(8):
        at = slice(i * rows, (i + 1) * rows)
        e = mine_ref[at]
        for ref, scale in zip(coded_refs, scales):
            e = e + unpack(ref, rows, i).astype(jnp.float32) * scale
        sq = e * e
        sq_ref[at] = sq
        total = total + jnp.sum(sq, axis=0, keepdims=True)
    sum_ref[...] = total


def product_kernel(masks, n_layer, n_row, n_col, ids_ref, *refs):
    n_slots, n_held = n_layer // 2, 2 * len(masks)
    b_refs, a_refs = refs[:4], refs[4 : 4 + n_held]
    out_refs = refs[4 + n_held : -2]
    where_ref, lhs_ref = refs[-2:]
    layer, row, col = (lax.axis_index(n) for n in ("layer", "row", "col"))
    per, per_row = IB // n_layer, n_col // n_row // 2
    capacity, block, depth = a_refs[0].shape
    rhs = []
    for k in range(n_held):
        other, place = k % 2, k // 2
        for i in range(IB + 1):
            where_ref[k, i] = -1
        for n in range(capacity):
            where_ref[k, ids_ref[k, n]] = n
        pair = (col ^ masks[place]) // 2
        start = (((pair // per_row) ^ row) * per_row + pair % per_row) * depth
        at = pl.ds(pl.multiple_of(start, depth), depth)
        rhs.append(jnp.concatenate([b_refs[2 * m + other][at, :] for m in range(2)], axis=1))
    rhs = jnp.concatenate(rhs, axis=0)
    width = rhs.shape[1] // 2
    for slot in range(n_slots):
        for sub in range(per):
            block_row = (layer ^ (2 * slot)) * per + sub
            for k in range(n_held):
                n = where_ref[k, block_row]
                a = a_refs[k][jnp.maximum(n, 0)]
                lhs_ref[slot, sub * block : (sub + 1) * block, k * depth : (k + 1) * depth] = (
                    jnp.where(n >= 0, a, jnp.zeros_like(a))
                )
        out = jnp.dot(lhs_ref[slot], rhs, preferred_element_type=jnp.float32)
        for m in range(2):
            part, out_ref = out[:, m * width : (m + 1) * width], out_refs[2 * slot + m]
            if slot or m:
                pack(part, out_ref)
            else:
                out_ref[...] = part


def products(masks, ids, b_refs, panels):
    n_layer, n_row, n_col = (lax.axis_size(a) for a in ("layer", "row", "col"))
    _, block, depth = panels[0].shape
    rows, n_slots, width = IB // n_layer * block, n_layer // 2, b_refs[0].shape[1]
    ins = [*b_refs, *panels]
    return pl.pallas_call(
        functools.partial(product_kernel, masks, n_layer, n_row, n_col),
        out_shape=[pltpu.VMEM((rows, width), jnp.float32)]
        + [pltpu.VMEM((rows // 8 * 5 + 8, width), jnp.int32)] * (2 * n_slots - 1),
        in_specs=[SMEM] + [VMEM] * len(ins),
        out_specs=[VMEM] * (2 * n_slots),
        scratch_shapes=[
            pltpu.SMEM((len(panels), IB + 1), jnp.int32),
            pltpu.VMEM((n_slots, rows, len(panels) * depth), jnp.bfloat16),
        ],
        name="partial_rows",
    )(ids, *(pin(x) for x in ins))


def body(a_blocks, a_rows, a_count, b_panel):
    n_layer, n_row, n_col = (lax.axis_size(a) for a in ("layer", "row", "col"))
    _, capacity, block, _ = a_blocks.shape

    def other(x):
        return xor_permute(x, "layer", 1)

    masks, panels = [0], [a_blocks[0]]
    valid = jnp.arange(capacity, dtype=jnp.int32)[None, :] < a_count[:, None]
    ids = jnp.where(valid, a_rows, IB)
    ids = jnp.concatenate([ids, other(ids)])
    bit = n_col // 2
    while bit > 1:
        panels = panels + [xor_permute(p, "col", bit) for p in panels]
        ids = jnp.concatenate([ids, xor_permute(ids, "col", bit)])
        masks = masks + [m ^ bit for m in masks]
        bit //= 2

    b_rows = [b_panel]
    bit = 1
    while bit < n_row:
        b_rows = b_rows + [xor_permute(b, "row", bit) for b in b_rows]
        bit *= 2
    b_rows = jnp.concatenate(b_rows).reshape(-1, 2, *b_panel.shape[-1:] * 2)
    parity = lax.axis_index("col") % 2
    b_mine, b_near = (
        lax.dynamic_index_in_dim(b_rows, p, 1, False).reshape(-1, b_panel.shape[1])
        for p in (parity, 1 - parity)
    )
    b_refs = [b_mine, other(b_mine), xor_permute(b_near, "col", 1)]

    far, ids, b_refs = lax.optimization_barrier((panels[1:], ids, b_refs))
    panels[1:] = far
    b_refs.append(other(b_refs[2]))
    panels = [x for p in panels for x in (p, other(p))]
    parts = products(masks, ids, b_refs, panels)

    parts = [parts[0]] + [grid_permute(parts[k], (2 * (k // 2), 0, k % 2)) for k in range(1, n_layer)]
    sq, col_sum = pl.pallas_call(
        square_kernel,
        out_shape=(
            pltpu.VMEM(parts[0].shape, jnp.float32),
            pltpu.VMEM((1, parts[0].shape[1]), jnp.float32),
        ),
        in_specs=[VMEM] * len(parts),
        out_specs=(VMEM, VMEM),
        name="squares",
    )(*(pin(x) for x in parts))

    col_sum = sum_over_devices(col_sum)
    scale = 1.0 / (col_sum * (1.0 / (n_row * IB * block)) + 1e-06)
    return (sq * scale)[None]


def solution(mesh):
    return jax.shard_map(
        body,
        mesh=mesh,
        in_specs=(
            P(("layer", "row", "col"), None, None, None),
            P(("layer", "row", "col"), None),
            P(("layer", "row", "col")),
            P(("layer", "row"), "col"),
        ),
        out_specs=P("row", "layer", "col"),
        check_vma=False,
    )
```

```python
import functools

import jax
import jax.numpy as jnp
import numpy as np
from jax import lax
from jax.experimental import pallas as pl
from jax.experimental.pallas import tpu as pltpu
from jax.sharding import PartitionSpec as P

IB = 16
AXES = ("layer", "row", "col")
BITS = 20
VMEM = pl.BlockSpec(memory_space=pltpu.VMEM)
SMEM = pl.BlockSpec(memory_space=pltpu.SMEM)


def pin(x):
    return pltpu.with_memory_space_constraint(x, pltpu.VMEM)


def xor_permute(x, axis, mask):
    return lax.ppermute(x, axis, [(i, i ^ mask) for i in range(lax.axis_size(axis))])


def grid_permute(x, masks, other_masks=None):
    sizes = [lax.axis_size(a) for a in AXES]
    pairs = []
    for source, at in enumerate(np.ndindex(*sizes)):
        by = other_masks if other_masks and at[0] % 2 else masks
        target = [i ^ m for i, m in zip(at, by, strict=True)]
        pairs.append((source, int(np.ravel_multi_index(target, sizes))))
    return lax.ppermute(x, AXES, pairs)


def sum_over_devices(x):
    n_layer, n_row, _ = (lax.axis_size(a) for a in AXES)
    chips = [(i, j, 0) for i in range(0, n_layer, 2) for j in range(n_row)][:0:-1]
    got = [grid_permute(x, chips.pop(0))] if len(chips) % 2 else []
    x = x + xor_permute(x, "layer", 1)
    got += [grid_permute(x, *chips[k : k + 2]) for k in range(0, len(chips), 2)]
    got = sum(got)
    return x + (got + xor_permute(got, "layer", 1))


def power_of_two(k):
    scale = jnp.ones(k.shape, jnp.float32)
    for b in range(7):
        factor = jnp.where(k < 0, 2.0 ** -(2**b), 2.0 ** (2**b))
        scale = jnp.where((jnp.abs(k) >> b) & 1 == 1, scale * factor, scale)
    return scale


def pack(part, out_ref):
    top = jnp.max(jnp.abs(part), axis=0, keepdims=True)
    k = jnp.clip(jnp.ceil(jnp.log2(top) + 0.01), -100.0, 126.0).astype(jnp.int32)
    q = jnp.floor(part * power_of_two(BITS - 1 - k) + 0.5).astype(jnp.int32)
    rows = part.shape[0] // 8
    q = [q[i * rows : (i + 1) * rows] for i in range(8)]
    low = [
        q[5] & 4095,
        ((q[5] >> 12) & 255) | ((q[6] & 15) << 8),
        (q[6] >> 4) & 4095,
        ((q[6] >> 16) & 15) | ((q[7] & 255) << 4),
        (q[7] >> 8) & 4095,
    ]
    for i in range(5):
        out_ref[i * rows : (i + 1) * rows] = (q[i] << 12) | low[i]
    out_ref[5 * rows :] = jnp.broadcast_to(k, (8, part.shape[1]))


def unpack(ref, rows, i):
    w = [ref[j * rows : (j + 1) * rows] for j in ([i] if i < 5 else range(5))]
    if i < 5:
        return w[0] >> 12
    if i == 5:
        return (w[0] & 4095) | ((w[1] << 24) >> 12)
    if i == 6:
        return ((w[1] >> 8) & 15) | ((w[2] & 4095) << 4) | ((w[3] << 28) >> 12)
    return ((w[3] >> 4) & 255) | ((w[4] << 20) >> 12)


def square_kernel(mine_ref, *refs):
    coded_refs, (sq_ref, sum_ref) = refs[:-2], refs[-2:]
    rows = mine_ref.shape[0] // 8
    scales = [power_of_two(ref[5 * rows : 5 * rows + 1] - (BITS - 1)) for ref in coded_refs]
    total = jnp.zeros(sum_ref.shape, jnp.float32)
    for i in range(8):
        at = slice(i * rows, (i + 1) * rows)
        e = mine_ref[at]
        for ref, scale in zip(coded_refs, scales):
            e = e + unpack(ref, rows, i).astype(jnp.float32) * scale
        sq = e * e
        sq_ref[at] = sq
        total = total + jnp.sum(sq, axis=0, keepdims=True)
    sum_ref[...] = total


def product_kernel(masks, n_layer, n_row, n_col, ids_ref, *refs):
    n_slots, n_held = n_layer // 2, 2 * len(masks)
    mine_refs, near_refs = refs[:2], refs[2 : 2 + 2 * n_row]
    a_refs, out_refs = refs[2 + 2 * n_row : 2 + 2 * n_row + n_held], refs[2 + 2 * n_row + n_held : -2]
    where_ref, lhs_ref = refs[-2:]
    layer, row, col = (lax.axis_index(n) for n in ("layer", "row", "col"))
    per, per_row = IB // n_layer, n_col // n_row
    capacity, block, depth = a_refs[0].shape
    rhs = []
    for k in range(n_held):
        other, place = k % 2, k // 2
        for i in range(IB + 1):
            where_ref[k, i] = -1
        for n in range(capacity):
            where_ref[k, ids_ref[k, n]] = n
        panel = col ^ masks[place]
        at = panel % per_row * depth
        owner = (panel // per_row) ^ row
        start = pl.multiple_of(owner * (per_row * depth) + at, depth)
        mine = mine_refs[other][pl.ds(start, depth), :]
        at = pl.ds(pl.multiple_of(at, depth), depth)
        near = near_refs[other][at, :]
        for i in range(1, n_row):
            near = jnp.where(owner == i, near_refs[2 * i + other][at, :], near)
        rhs.append(jnp.concatenate([mine, near], axis=1))
    rhs = jnp.concatenate(rhs, axis=0)
    width = rhs.shape[1] // 2
    for slot in range(n_slots):
        for sub in range(per):
            block_row = (layer ^ (2 * slot)) * per + sub
            for k in range(n_held):
                n = where_ref[k, block_row]
                a = a_refs[k][jnp.maximum(n, 0)]
                lhs_ref[slot, sub * block : (sub + 1) * block, k * depth : (k + 1) * depth] = (
                    jnp.where(n >= 0, a, jnp.zeros_like(a))
                )
        out = jnp.dot(lhs_ref[slot], rhs, preferred_element_type=jnp.float32)
        for m in range(2):
            part, out_ref = out[:, m * width : (m + 1) * width], out_refs[2 * slot + m]
            if slot or m:
                pack(part, out_ref)
            else:
                out_ref[...] = part


def products(masks, ids, b_refs, panels):
    n_layer, n_row, n_col = (lax.axis_size(a) for a in ("layer", "row", "col"))
    _, block, depth = panels[0].shape
    rows, n_slots, width = IB // n_layer * block, n_layer // 2, b_refs[0].shape[1]
    ins = [*b_refs, *panels]
    return pl.pallas_call(
        functools.partial(product_kernel, masks, n_layer, n_row, n_col),
        out_shape=[pltpu.VMEM((rows, width), jnp.float32)]
        + [pltpu.VMEM((rows // 8 * 5 + 8, width), jnp.int32)] * (2 * n_slots - 1),
        in_specs=[SMEM] + [VMEM] * len(ins),
        out_specs=[VMEM] * (2 * n_slots),
        scratch_shapes=[
            pltpu.SMEM((len(panels), IB + 1), jnp.int32),
            pltpu.VMEM((n_slots, rows, len(panels) * depth), jnp.bfloat16),
        ],
        name="partial_rows",
    )(ids, *(pin(x) for x in ins))


def body(a_blocks, a_rows, a_count, b_panel):
    n_layer, n_row, n_col = (lax.axis_size(a) for a in ("layer", "row", "col"))
    _, capacity, block, _ = a_blocks.shape

    def other(x):
        return xor_permute(x, "layer", 1)

    masks, panels = [0], [a_blocks[0]]
    valid = jnp.arange(capacity, dtype=jnp.int32)[None, :] < a_count[:, None]
    ids = jnp.where(valid, a_rows, IB)
    ids = jnp.concatenate([ids, other(ids)])
    bit = n_col // 2
    while bit > 1:
        panels = panels + [xor_permute(p, "col", bit) for p in panels]
        ids = jnp.concatenate([ids, xor_permute(ids, "col", bit)])
        masks = masks + [m ^ bit for m in masks]
        bit //= 2

    own_other = other(panels[0])
    b_panel, own_other = lax.optimization_barrier((b_panel, own_other))

    b_rows = [[b_panel, xor_permute(b_panel, "col", 1)]]
    bit = 1
    while bit < n_row:
        b_rows = b_rows + [[xor_permute(b, "row", bit) for b in pair] for pair in b_rows]
        bit *= 2

    mine = jnp.concatenate([pair[0] for pair in b_rows])
    mine = [mine, other(mine)]
    near = [pair[1] for pair in b_rows]
    own = a_blocks[0]
    far, ids, mine, near, own_other = lax.optimization_barrier(
        (panels[1:], ids, mine, near, own_other)
    )
    near = [x for b in near for x in (b, other(b))]
    panels = [own, own_other] + [x for p in far for x in (p, other(p))]
    b_refs = mine + near
    parts = products(masks, ids, b_refs, panels)

    parts = [parts[0]] + [grid_permute(parts[k], (2 * (k // 2), 0, k % 2)) for k in range(1, n_layer)]
    sq, col_sum = pl.pallas_call(
        square_kernel,
        out_shape=(
            pltpu.VMEM(parts[0].shape, jnp.float32),
            pltpu.VMEM((1, parts[0].shape[1]), jnp.float32),
        ),
        in_specs=[VMEM] * len(parts),
        out_specs=(VMEM, VMEM),
        name="squares",
    )(*(pin(x) for x in parts))

    col_sum = sum_over_devices(col_sum)
    scale = 1.0 / (col_sum * (1.0 / (n_row * IB * block)) + 1e-06)
    return (sq * scale)[None]


def solution(mesh):
    return jax.shard_map(
        body,
        mesh=mesh,
        in_specs=(
            P(("layer", "row", "col"), None, None, None),
            P(("layer", "row", "col"), None),
            P(("layer", "row", "col")),
            P(("layer", "row"), "col"),
        ),
        out_specs=P("row", "layer", "col"),
        check_vma=False,
    )
```

```python
import functools

import jax
import jax.numpy as jnp
import numpy as np
from jax import lax
from jax.experimental import pallas as pl
from jax.experimental.pallas import tpu as pltpu
from jax.sharding import PartitionSpec as P

IB = 16
AXES = ("layer", "row", "col")
BITS, VALUES, WORDS = 18, 16, 9
VMEM = pl.BlockSpec(memory_space=pltpu.VMEM)
SMEM = pl.BlockSpec(memory_space=pltpu.SMEM)


def pin(x):
    return pltpu.with_memory_space_constraint(x, pltpu.VMEM)


def xor_permute(x, axis, mask):
    return lax.ppermute(x, axis, [(i, i ^ mask) for i in range(lax.axis_size(axis))])


def grid_permute(x, masks, other_masks=None):
    sizes = [lax.axis_size(a) for a in AXES]
    pairs = []
    for source, at in enumerate(np.ndindex(*sizes)):
        by = other_masks if other_masks and at[0] % 2 else masks
        target = [i ^ m for i, m in zip(at, by, strict=True)]
        pairs.append((source, int(np.ravel_multi_index(target, sizes))))
    return lax.ppermute(x, AXES, pairs)


def sum_over_devices(x):
    n_layer, n_row, _ = (lax.axis_size(a) for a in AXES)
    chips = [(i, j, 0) for i in range(0, n_layer, 2) for j in range(n_row)][:0:-1]
    got = [grid_permute(x, chips.pop(0))] if len(chips) % 2 else []
    x = x + xor_permute(x, "layer", 1)
    got += [grid_permute(x, *chips[k : k + 2]) for k in range(0, len(chips), 2)]
    got = sum(got)
    return x + (got + xor_permute(got, "layer", 1))


def power_of_two(k):
    scale = jnp.ones(k.shape, jnp.float32)
    for b in range(7):
        factor = jnp.where(k < 0, 2.0 ** -(2**b), 2.0 ** (2**b))
        scale = jnp.where((jnp.abs(k) >> b) & 1 == 1, scale * factor, scale)
    return scale


def low_fields(i):
    fields, at, bit = [], (i - WORDS) * BITS, 0
    while bit < BITS:
        word, to = divmod(at, 32 - BITS)
        bits = min(BITS - bit, 32 - BITS - to)
        fields.append((bit, word, to, bits))
        at, bit = at + bits, bit + bits
    return fields


def pack(part, out_ref):
    top = jnp.max(jnp.abs(part), axis=0, keepdims=True)
    k = jnp.clip(jnp.ceil(jnp.log2(top) + 0.01), -100.0, 126.0).astype(jnp.int32)
    q = jnp.floor(part * power_of_two(BITS - 1 - k) + 0.5).astype(jnp.int32)
    rows = part.shape[0] // VALUES
    q = [q[i * rows : (i + 1) * rows] for i in range(VALUES)]
    words = [q[j] << (32 - BITS) for j in range(WORDS)]
    for i in range(WORDS, VALUES):
        for bit, word, to, bits in low_fields(i):
            words[word] = words[word] | (((q[i] >> bit) & ((1 << bits) - 1)) << to)
    for j in range(WORDS):
        out_ref[j * rows : (j + 1) * rows] = words[j]
    out_ref[WORDS * rows :] = jnp.broadcast_to(k, (8, part.shape[1]))


def unpack(ref, rows, i):
    if i < WORDS:
        return ref[i * rows : (i + 1) * rows] >> (32 - BITS)
    total = None
    for bit, word, to, bits in low_fields(i):
        w = ref[word * rows : (word + 1) * rows]
        if bit + bits == BITS:
            w = ((w << (32 - to - bits)) >> (32 - bits)) << bit
        else:
            w = ((w >> to) & ((1 << bits) - 1)) << bit
        total = w if total is None else total | w
    return total


def square_kernel(mine_ref, *refs):
    coded_refs, (sq_ref, sum_ref) = refs[:-2], refs[-2:]
    rows = mine_ref.shape[0] // VALUES
    scales = [power_of_two(ref[WORDS * rows : WORDS * rows + 1] - (BITS - 1)) for ref in coded_refs]
    total = jnp.zeros(sum_ref.shape, jnp.float32)
    for i in range(VALUES):
        at = slice(i * rows, (i + 1) * rows)
        e = mine_ref[at]
        for ref, scale in zip(coded_refs, scales):
            e = e + unpack(ref, rows, i).astype(jnp.float32) * scale
        sq = e * e
        sq_ref[at] = sq
        total = total + jnp.sum(sq, axis=0, keepdims=True)
    sum_ref[...] = total


def product_kernel(masks, n_layer, n_row, n_col, ids_ref, *refs):
    n_slots, n_held = n_layer // 2, 2 * len(masks)
    mine_refs, near_refs = refs[:2], refs[2 : 2 + 2 * n_row]
    a_refs, out_refs = refs[2 + 2 * n_row : 2 + 2 * n_row + n_held], refs[2 + 2 * n_row + n_held : -2]
    where_ref, lhs_ref = refs[-2:]
    layer, row, col = (lax.axis_index(n) for n in ("layer", "row", "col"))
    per, per_row = IB // n_layer, n_col // n_row
    capacity, block, depth = a_refs[0].shape
    rhs = []
    for k in range(n_held):
        other, place = k % 2, k // 2
        for i in range(IB + 1):
            where_ref[k, i] = -1
        for n in range(capacity):
            where_ref[k, ids_ref[k, n]] = n
        panel = col ^ masks[place]
        at = panel % per_row * depth
        owner = (panel // per_row) ^ row
        start = pl.multiple_of(owner * (per_row * depth) + at, depth)
        mine = mine_refs[other][pl.ds(start, depth), :]
        at = pl.ds(pl.multiple_of(at, depth), depth)
        near = near_refs[other][at, :]
        for i in range(1, n_row):
            near = jnp.where(owner == i, near_refs[2 * i + other][at, :], near)
        rhs.append(jnp.concatenate([mine, near], axis=1))
    rhs = jnp.concatenate(rhs, axis=0)
    width = rhs.shape[1] // 2
    for slot in range(n_slots):
        for sub in range(per):
            block_row = (layer ^ (2 * slot)) * per + sub
            for k in range(n_held):
                n = where_ref[k, block_row]
                a = a_refs[k][jnp.maximum(n, 0)]
                lhs_ref[slot, sub * block : (sub + 1) * block, k * depth : (k + 1) * depth] = (
                    jnp.where(n >= 0, a, jnp.zeros_like(a))
                )
        out = jnp.dot(lhs_ref[slot], rhs, preferred_element_type=jnp.float32)
        for m in range(2):
            part, out_ref = out[:, m * width : (m + 1) * width], out_refs[2 * slot + m]
            if slot or m:
                pack(part, out_ref)
            else:
                out_ref[...] = part


def products(masks, ids, b_refs, panels):
    n_layer, n_row, n_col = (lax.axis_size(a) for a in ("layer", "row", "col"))
    _, block, depth = panels[0].shape
    rows, n_slots, width = IB // n_layer * block, n_layer // 2, b_refs[0].shape[1]
    ins = [*b_refs, *panels]
    return pl.pallas_call(
        functools.partial(product_kernel, masks, n_layer, n_row, n_col),
        out_shape=[pltpu.VMEM((rows, width), jnp.float32)]
        + [pltpu.VMEM((rows // VALUES * WORDS + 8, width), jnp.int32)] * (2 * n_slots - 1),
        in_specs=[SMEM] + [VMEM] * len(ins),
        out_specs=[VMEM] * (2 * n_slots),
        scratch_shapes=[
            pltpu.SMEM((len(panels), IB + 1), jnp.int32),
            pltpu.VMEM((n_slots, rows, len(panels) * depth), jnp.bfloat16),
        ],
        name="partial_rows",
    )(ids, *(pin(x) for x in ins))


def body(a_blocks, a_rows, a_count, b_panel):
    n_layer, n_row, n_col = (lax.axis_size(a) for a in ("layer", "row", "col"))
    _, capacity, block, _ = a_blocks.shape

    def other(x):
        return xor_permute(x, "layer", 1)

    masks, panels = [0], [a_blocks[0]]
    valid = jnp.arange(capacity, dtype=jnp.int32)[None, :] < a_count[:, None]
    ids = jnp.where(valid, a_rows, IB)
    ids = jnp.concatenate([ids, other(ids)])
    bit = n_col // 2
    while bit > 1:
        panels = panels + [xor_permute(p, "col", bit) for p in panels]
        ids = jnp.concatenate([ids, xor_permute(ids, "col", bit)])
        masks = masks + [m ^ bit for m in masks]
        bit //= 2

    own_other = other(panels[0])
    b_panel, own_other = lax.optimization_barrier((b_panel, own_other))

    b_rows = [[b_panel, xor_permute(b_panel, "col", 1)]]
    bit = 1
    while bit < n_row:
        b_rows = b_rows + [[xor_permute(b, "row", bit) for b in pair] for pair in b_rows]
        bit *= 2

    mine = jnp.concatenate([pair[0] for pair in b_rows])
    mine = [mine, other(mine)]
    near = [pair[1] for pair in b_rows]
    own = a_blocks[0]
    far, ids, mine, near, own_other = lax.optimization_barrier(
        (panels[1:], ids, mine, near, own_other)
    )
    near = [x for b in near for x in (b, other(b))]
    panels = [own, own_other] + [x for p in far for x in (p, other(p))]
    b_refs = mine + near
    parts = products(masks, ids, b_refs, panels)

    parts = [parts[0]] + [grid_permute(parts[k], (2 * (k // 2), 0, k % 2)) for k in range(1, n_layer)]
    sq, col_sum = pl.pallas_call(
        square_kernel,
        out_shape=(
            pltpu.VMEM(parts[0].shape, jnp.float32),
            pltpu.VMEM((1, parts[0].shape[1]), jnp.float32),
        ),
        in_specs=[VMEM] * len(parts),
        out_specs=(VMEM, VMEM),
        name="squares",
    )(*(pin(x) for x in parts))

    col_sum = sum_over_devices(col_sum)
    scale = 1.0 / (col_sum * (1.0 / (n_row * IB * block)) + 1e-06)
    return (sq * scale)[None]


def solution(mesh):
    return jax.shard_map(
        body,
        mesh=mesh,
        in_specs=(
            P(("layer", "row", "col"), None, None, None),
            P(("layer", "row", "col"), None),
            P(("layer", "row", "col")),
            P(("layer", "row"), "col"),
        ),
        out_specs=P("row", "layer", "col"),
        check_vma=False,
    )
```

```python
import functools

import jax
import jax.numpy as jnp
import numpy as np
from jax import lax
from jax.experimental import pallas as pl
from jax.experimental.pallas import tpu as pltpu
from jax.sharding import PartitionSpec as P

IB = 16
AXES = ("layer", "row", "col")
BITS, VALUES, WORDS = 18, 16, 9
VMEM = pl.BlockSpec(memory_space=pltpu.VMEM)


def pin(x):
    return pltpu.with_memory_space_constraint(x, pltpu.VMEM)


def xor_permute(x, axis, mask):
    return lax.ppermute(x, axis, [(i, i ^ mask) for i in range(lax.axis_size(axis))])


def grid_permute(x, masks, other_masks=None):
    sizes = [lax.axis_size(a) for a in AXES]
    pairs = []
    for source, at in enumerate(np.ndindex(*sizes)):
        by = other_masks if other_masks and at[0] % 2 else masks
        target = [i ^ m for i, m in zip(at, by, strict=True)]
        pairs.append((source, int(np.ravel_multi_index(target, sizes))))
    return lax.ppermute(x, AXES, pairs)


def sum_over_devices(x):
    n_layer, n_row, _ = (lax.axis_size(a) for a in AXES)
    chips = [(i, j, 0) for i in range(0, n_layer, 2) for j in range(n_row)][:0:-1]
    got = [grid_permute(x, chips.pop(0))] if len(chips) % 2 else []
    x = x + xor_permute(x, "layer", 1)
    got += [grid_permute(x, *chips[k : k + 2]) for k in range(0, len(chips), 2)]
    got = sum(got)
    return x + (got + xor_permute(got, "layer", 1))


def power_of_two(k):
    scale = jnp.ones(k.shape, jnp.float32)
    for b in range(7):
        factor = jnp.where(k < 0, 2.0 ** -(2**b), 2.0 ** (2**b))
        scale = jnp.where((jnp.abs(k) >> b) & 1 == 1, scale * factor, scale)
    return scale


def low_fields(i):
    fields, at, bit = [], (i - WORDS) * BITS, 0
    while bit < BITS:
        word, to = divmod(at, 32 - BITS)
        bits = min(BITS - bit, 32 - BITS - to)
        fields.append((bit, word, to, bits))
        at, bit = at + bits, bit + bits
    return fields


def pack(part, out_ref):
    top = jnp.max(jnp.abs(part), axis=0, keepdims=True)
    k = jnp.clip(jnp.ceil(jnp.log2(top) + 0.01), -100.0, 126.0).astype(jnp.int32)
    q = jnp.floor(part * power_of_two(BITS - 1 - k) + 0.5).astype(jnp.int32)
    rows = part.shape[0] // VALUES
    q = [q[i * rows : (i + 1) * rows] for i in range(VALUES)]
    words = [q[j] << (32 - BITS) for j in range(WORDS)]
    for i in range(WORDS, VALUES):
        for bit, word, to, bits in low_fields(i):
            words[word] = words[word] | (((q[i] >> bit) & ((1 << bits) - 1)) << to)
    for j in range(WORDS):
        out_ref[j * rows : (j + 1) * rows] = words[j]
    out_ref[WORDS * rows :] = jnp.broadcast_to(k, (8, part.shape[1]))


def unpack(ref, rows, i):
    if i < WORDS:
        return ref[i * rows : (i + 1) * rows] >> (32 - BITS)
    total = None
    for bit, word, to, bits in low_fields(i):
        w = ref[word * rows : (word + 1) * rows]
        if bit + bits == BITS:
            w = ((w << (32 - to - bits)) >> (32 - bits)) << bit
        else:
            w = ((w >> to) & ((1 << bits) - 1)) << bit
        total = w if total is None else total | w
    return total


def square_kernel(mine_ref, *refs):
    coded_refs, (sq_ref, sum_ref) = refs[:-2], refs[-2:]
    rows = mine_ref.shape[0] // VALUES
    scales = [power_of_two(ref[WORDS * rows : WORDS * rows + 1] - (BITS - 1)) for ref in coded_refs]
    total = jnp.zeros(sum_ref.shape, jnp.float32)
    for i in range(VALUES):
        at = slice(i * rows, (i + 1) * rows)
        e = mine_ref[at]
        for ref, scale in zip(coded_refs, scales):
            e = e + unpack(ref, rows, i).astype(jnp.float32) * scale
        sq = e * e
        sq_ref[at] = sq
        total = total + jnp.sum(sq, axis=0, keepdims=True)
    sum_ref[...] = total


def product_kernel(masks, n_layer, n_row, n_col, lists_ref, *refs):
    n_slots, n_held = n_layer // 2, 2 * len(masks)
    mine_refs, near_refs = refs[:2], refs[2 : 2 + 2 * n_row]
    a_refs, out_refs = refs[2 + 2 * n_row : 2 + 2 * n_row + n_held], refs[2 + 2 * n_row + n_held : -1]
    lhs_ref = refs[-1]
    layer, row, col = (lax.axis_index(n) for n in ("layer", "row", "col"))
    per, per_row = IB // n_layer, n_col // n_row
    capacity, block, depth = a_refs[0].shape
    lists = lists_ref[...]
    lists = [[lists[k, h] for h in range(lists.shape[1])] for k in range(n_held)]
    rhs = []
    for k in range(n_held):
        other, place = k % 2, k // 2
        panel = col ^ masks[place]
        at = panel % per_row * depth
        owner = (panel // per_row) ^ row
        start = pl.multiple_of(owner * (per_row * depth) + at, depth)
        mine = mine_refs[other][pl.ds(start, depth), :]
        at = pl.ds(pl.multiple_of(at, depth), depth)
        near = near_refs[other][at, :]
        for i in range(1, n_row):
            near = jnp.where(owner == i, near_refs[2 * i + other][at, :], near)
        rhs.append(jnp.concatenate([mine, near], axis=1))
    rhs = jnp.concatenate(rhs, axis=0)
    width, parts = rhs.shape[1] // 2, []
    for slot in range(n_slots):
        for sub in range(per):
            block_row = (layer ^ (2 * slot)) * per + sub
            for k in range(n_held):
                word = lists[k][0]
                for h in range(1, len(lists[k])):
                    word = jnp.where(block_row // 8 == h, lists[k][h], word)
                n = (word >> (block_row % 8 * 4)) & 15
                a = a_refs[k][jnp.minimum(n, capacity - 1)]
                lhs_ref[slot, sub * block : (sub + 1) * block, k * depth : (k + 1) * depth] = (
                    jnp.where(n < capacity, a, jnp.zeros_like(a))
                )
        out = jnp.dot(lhs_ref[slot], rhs, preferred_element_type=jnp.float32)
        parts += [out[:, m * width : (m + 1) * width] for m in range(2)]
    out_refs[0][...] = parts[0]
    for k in range(1, 2 * n_slots - 1, 2):
        one, two = parts[k : k + 2]
        pack(jnp.where(layer % 2 == 0, one, two), out_refs[k])
        pack(jnp.where(layer % 2 == 0, two, one), out_refs[k + 1])
    pack(parts[-1], out_refs[-1])


def products(masks, lists, b_refs, panels):
    n_layer, n_row, n_col = (lax.axis_size(a) for a in ("layer", "row", "col"))
    _, block, depth = panels[0].shape
    rows, n_slots, width = IB // n_layer * block, n_layer // 2, b_refs[0].shape[1]
    ins = [lists, *b_refs, *panels]
    return pl.pallas_call(
        functools.partial(product_kernel, masks, n_layer, n_row, n_col),
        out_shape=[pltpu.VMEM((rows, width), jnp.float32)]
        + [pltpu.VMEM((rows // VALUES * WORDS + 8, width), jnp.int32)] * (2 * n_slots - 1),
        in_specs=[VMEM] * len(ins),
        out_specs=[VMEM] * (2 * n_slots),
        scratch_shapes=[
            pltpu.VMEM((n_slots, rows, len(panels) * depth), jnp.bfloat16),
        ],
        name="partial_rows",
    )(*(pin(x) for x in ins))


def whereabouts(a_rows, a_count):
    panels, capacity = a_rows.shape
    place = jnp.arange(capacity, dtype=jnp.int32)
    valid = place[None, :] < a_count[:, None]
    block_rows = jnp.arange(IB, dtype=jnp.int32)
    listed = (a_rows[:, :, None] == block_rows) & valid[:, :, None]
    places = capacity + jnp.sum(jnp.where(listed, place[:, None] - capacity, 0), axis=1)
    return jnp.sum((places << (block_rows % 8 * 4)).reshape(panels, IB // 8, 8), axis=2)


def body(a_blocks, a_rows, a_count, b_panel):
    n_layer, n_row, n_col = (lax.axis_size(a) for a in ("layer", "row", "col"))
    _, capacity, block, _ = a_blocks.shape

    def other(x):
        return xor_permute(x, "layer", 1)

    masks, panels = [0], [a_blocks[0]]
    lists = whereabouts(a_rows, a_count)
    lists = jnp.concatenate([lists, other(lists)])
    bit = n_col // 2
    while bit > 1:
        panels = panels + [xor_permute(p, "col", bit) for p in panels]
        lists = jnp.concatenate([lists, xor_permute(lists, "col", bit)])
        masks = masks + [m ^ bit for m in masks]
        bit //= 2

    own_other = other(panels[0])
    b_panel, own_other = lax.optimization_barrier((b_panel, own_other))

    b_rows = [[b_panel, xor_permute(b_panel, "col", 1)]]
    bit = 1
    while bit < n_row:
        b_rows = b_rows + [[xor_permute(b, "row", bit) for b in pair] for pair in b_rows]
        bit *= 2

    mine = jnp.concatenate([pair[0] for pair in b_rows])
    mine = [mine, other(mine)]
    near = [pair[1] for pair in b_rows]
    own = a_blocks[0]
    far, lists, mine, near, own_other = lax.optimization_barrier(
        (panels[1:], lists, mine, near, own_other)
    )
    near = [x for b in near for x in (b, other(b))]
    panels = [own, own_other] + [x for p in far for x in (p, other(p))]
    b_refs = mine + near
    parts = products(masks, lists, b_refs, panels)

    masks = [(2 * (k // 2), 0, k % 2) for k in range(n_layer)]
    swaps = [0] + [k + 1 if k % 2 else k - 1 for k in range(1, n_layer - 1)] + [n_layer - 1]
    parts = [parts[0]] + [
        grid_permute(parts[k], masks[k], masks[swaps[k]]) for k in range(1, n_layer)
    ]
    sq, col_sum = pl.pallas_call(
        square_kernel,
        out_shape=(
            pltpu.VMEM(parts[0].shape, jnp.float32),
            pltpu.VMEM((1, parts[0].shape[1]), jnp.float32),
        ),
        in_specs=[VMEM] * len(parts),
        out_specs=(VMEM, VMEM),
        name="squares",
    )(*(pin(x) for x in parts))

    col_sum = sum_over_devices(col_sum)
    scale = 1.0 / (col_sum * (1.0 / (n_row * IB * block)) + 1e-06)
    return (sq * scale)[None]


def solution(mesh):
    return jax.shard_map(
        body,
        mesh=mesh,
        in_specs=(
            P(("layer", "row", "col"), None, None, None),
            P(("layer", "row", "col"), None),
            P(("layer", "row", "col")),
            P(("layer", "row"), "col"),
        ),
        out_specs=P("row", "layer", "col"),
        check_vma=False,
    )
```

```python
import functools

import jax
import jax.numpy as jnp
import numpy as np
from jax import lax
from jax.experimental import pallas as pl
from jax.experimental.pallas import tpu as pltpu
from jax.sharding import PartitionSpec as P

IB = 16
AXES = ("layer", "row", "col")
BITS, VALUES, WORDS = 18, 16, 9
VMEM = pl.BlockSpec(memory_space=pltpu.VMEM)


def pin(x):
    return pltpu.with_memory_space_constraint(x, pltpu.VMEM)


def xor_permute(x, axis, mask):
    return lax.ppermute(x, axis, [(i, i ^ mask) for i in range(lax.axis_size(axis))])


def grid_permute(x, masks, other_masks=None):
    sizes = [lax.axis_size(a) for a in AXES]
    pairs = []
    for source, at in enumerate(np.ndindex(*sizes)):
        by = other_masks if other_masks and at[0] % 2 else masks
        target = [i ^ m for i, m in zip(at, by, strict=True)]
        pairs.append((source, int(np.ravel_multi_index(target, sizes))))
    return lax.ppermute(x, AXES, pairs)


def sum_over_devices(x):
    n_layer, n_row, _ = (lax.axis_size(a) for a in AXES)
    chips = [(i, j, 0) for i in range(0, n_layer, 2) for j in range(n_row)][:0:-1]
    got = [grid_permute(x, chips.pop(0))] if len(chips) % 2 else []
    x = x + xor_permute(x, "layer", 1)
    got += [grid_permute(x, *chips[k : k + 2]) for k in range(0, len(chips), 2)]
    got = sum(got)
    return x + (got + xor_permute(got, "layer", 1))


def power_of_two(k):
    scale = jnp.ones(k.shape, jnp.float32)
    for b in range(7):
        factor = jnp.where(k < 0, 2.0 ** -(2**b), 2.0 ** (2**b))
        scale = jnp.where((jnp.abs(k) >> b) & 1 == 1, scale * factor, scale)
    return scale


def low_fields(i):
    fields, at, bit = [], (i - WORDS) * BITS, 0
    while bit < BITS:
        word, to = divmod(at, 32 - BITS)
        bits = min(BITS - bit, 32 - BITS - to)
        fields.append((bit, word, to, bits))
        at, bit = at + bits, bit + bits
    return fields


def pack(part, out_ref):
    top = jnp.max(jnp.abs(part), axis=0, keepdims=True)
    k = jnp.clip(jnp.ceil(jnp.log2(top) + 0.01), -100.0, 126.0).astype(jnp.int32)
    q = jnp.floor(part * power_of_two(BITS - 1 - k) + 0.5).astype(jnp.int32)
    rows = part.shape[0] // VALUES
    q = [q[i * rows : (i + 1) * rows] for i in range(VALUES)]
    words = [q[j] << (32 - BITS) for j in range(WORDS)]
    for i in range(WORDS, VALUES):
        for bit, word, to, bits in low_fields(i):
            words[word] = words[word] | (((q[i] >> bit) & ((1 << bits) - 1)) << to)
    for j in range(WORDS):
        out_ref[j * rows : (j + 1) * rows] = words[j]
    out_ref[WORDS * rows :] = jnp.broadcast_to(k, (8, part.shape[1]))


def unpack(ref, rows, i):
    if i < WORDS:
        return ref[i * rows : (i + 1) * rows] >> (32 - BITS)
    total = None
    for bit, word, to, bits in low_fields(i):
        w = ref[word * rows : (word + 1) * rows]
        if bit + bits == BITS:
            w = ((w << (32 - to - bits)) >> (32 - bits)) << bit
        else:
            w = ((w >> to) & ((1 << bits) - 1)) << bit
        total = w if total is None else total | w
    return total


def square_kernel(mine_ref, *refs):
    coded_refs, (sq_ref, sum_ref) = refs[:-2], refs[-2:]
    rows = mine_ref.shape[0] // VALUES
    scales = [power_of_two(ref[WORDS * rows : WORDS * rows + 1] - (BITS - 1)) for ref in coded_refs]
    total = jnp.zeros(sum_ref.shape, jnp.float32)
    for i in range(VALUES):
        at = slice(i * rows, (i + 1) * rows)
        e = mine_ref[at]
        for ref, scale in zip(coded_refs, scales):
            e = e + unpack(ref, rows, i).astype(jnp.float32) * scale
        sq = e * e
        sq_ref[at] = sq
        total = total + jnp.sum(sq, axis=0, keepdims=True)
    sum_ref[...] = total


def places(listed):
    words = []
    for h in range(IB // 8):
        word = sum(8 << (4 * i) for i in range(8)) - (1 << 32)
        for n, block_row in enumerate(listed):
            bits = (n ^ 8) << (block_row % 8 * 4)
            word = word ^ jnp.where(block_row // 8 == h, bits, 0)
        words.append(word)
    return words


def product_kernel(masks, n_layer, n_row, n_col, lists_ref, *refs):
    n_slots, n_held = n_layer // 2, 2 * len(masks)
    mine_refs, near_refs = refs[:2], refs[2 : 2 + 2 * n_row]
    a_refs, out_refs = refs[2 + 2 * n_row : 2 + 2 * n_row + n_held], refs[2 + 2 * n_row + n_held : -1]
    lhs_ref = refs[-1]
    layer, row, col = (lax.axis_index(n) for n in ("layer", "row", "col"))
    per, per_row = IB // n_layer, n_col // n_row
    capacity, block, depth = a_refs[0].shape
    lists = lists_ref[...]
    lists = [places([lists[k, n] for n in range(capacity)]) for k in range(n_held)]
    rhs = []
    for k in range(n_held):
        other, place = k % 2, k // 2
        panel = col ^ masks[place]
        at = panel % per_row * depth
        owner = (panel // per_row) ^ row
        start = pl.multiple_of(owner * (per_row * depth) + at, depth)
        mine = mine_refs[other][pl.ds(start, depth), :]
        at = pl.ds(pl.multiple_of(at, depth), depth)
        near = near_refs[other][at, :]
        for i in range(1, n_row):
            near = jnp.where(owner == i, near_refs[2 * i + other][at, :], near)
        rhs.append(jnp.concatenate([mine, near], axis=1))
    rhs = jnp.concatenate(rhs, axis=0)
    width, parts = rhs.shape[1] // 2, []
    for slot in range(n_slots):
        for sub in range(per):
            block_row = (layer ^ (2 * slot)) * per + sub
            for k in range(n_held):
                word = lists[k][0]
                for h in range(1, len(lists[k])):
                    word = jnp.where(block_row // 8 == h, lists[k][h], word)
                n = (word >> (block_row % 8 * 4)) & 15
                a = a_refs[k][jnp.minimum(n, capacity - 1)]
                lhs_ref[slot, sub * block : (sub + 1) * block, k * depth : (k + 1) * depth] = (
                    jnp.where(n < capacity, a, jnp.zeros_like(a))
                )
        out = jnp.dot(lhs_ref[slot], rhs, preferred_element_type=jnp.float32)
        parts += [out[:, m * width : (m + 1) * width] for m in range(2)]
    out_refs[0][...] = parts[0]
    for k in range(1, 2 * n_slots - 1, 2):
        one, two = parts[k : k + 2]
        pack(jnp.where(layer % 2 == 0, one, two), out_refs[k])
        pack(jnp.where(layer % 2 == 0, two, one), out_refs[k + 1])
    pack(parts[-1], out_refs[-1])


def products(masks, lists, b_refs, panels):
    n_layer, n_row, n_col = (lax.axis_size(a) for a in ("layer", "row", "col"))
    _, block, depth = panels[0].shape
    rows, n_slots, width = IB // n_layer * block, n_layer // 2, b_refs[0].shape[1]
    ins = [lists, *b_refs, *panels]
    return pl.pallas_call(
        functools.partial(product_kernel, masks, n_layer, n_row, n_col),
        out_shape=[pltpu.VMEM((rows, width), jnp.float32)]
        + [pltpu.VMEM((rows // VALUES * WORDS + 8, width), jnp.int32)] * (2 * n_slots - 1),
        in_specs=[VMEM] * len(ins),
        out_specs=[VMEM] * (2 * n_slots),
        scratch_shapes=[
            pltpu.VMEM((n_slots, rows, len(panels) * depth), jnp.bfloat16),
        ],
        name="partial_rows",
    )(*(pin(x) for x in ins))


def body(a_blocks, a_rows, a_count, b_panel):
    n_layer, n_row, n_col = (lax.axis_size(a) for a in ("layer", "row", "col"))
    _, capacity, block, _ = a_blocks.shape

    def other(x):
        return xor_permute(x, "layer", 1)

    masks, panels = [0], [a_blocks[0]]
    valid = jnp.arange(capacity, dtype=jnp.int32)[None, :] < a_count[:, None]
    lists = jnp.where(valid, a_rows, IB)
    lists = jnp.concatenate([lists, other(lists)])
    bit = n_col // 2
    while bit > 1:
        panels = panels + [xor_permute(p, "col", bit) for p in panels]
        lists = jnp.concatenate([lists, xor_permute(lists, "col", bit)])
        masks = masks + [m ^ bit for m in masks]
        bit //= 2

    own_other = other(panels[0])
    b_panel, own_other = lax.optimization_barrier((b_panel, own_other))

    b_rows = [[b_panel, xor_permute(b_panel, "col", 1)]]
    bit = 1
    while bit < n_row:
        b_rows = b_rows + [[xor_permute(b, "row", bit) for b in pair] for pair in b_rows]
        bit *= 2

    mine = jnp.concatenate([pair[0] for pair in b_rows])
    mine = [mine, other(mine)]
    near = [pair[1] for pair in b_rows]
    own = a_blocks[0]
    far, lists, mine, near, own_other = lax.optimization_barrier(
        (panels[1:], lists, mine, near, own_other)
    )
    near = [x for b in near for x in (b, other(b))]
    panels = [own, own_other] + [x for p in far for x in (p, other(p))]
    b_refs = mine + near
    parts = products(masks, lists, b_refs, panels)

    masks = [(2 * (k // 2), 0, k % 2) for k in range(n_layer)]
    swaps = [0] + [k + 1 if k % 2 else k - 1 for k in range(1, n_layer - 1)] + [n_layer - 1]
    parts = [parts[0]] + [
        grid_permute(parts[k], masks[k], masks[swaps[k]]) for k in range(1, n_layer)
    ]
    sq, col_sum = pl.pallas_call(
        square_kernel,
        out_shape=(
            pltpu.VMEM(parts[0].shape, jnp.float32),
            pltpu.VMEM((1, parts[0].shape[1]), jnp.float32),
        ),
        in_specs=[VMEM] * len(parts),
        out_specs=(VMEM, VMEM),
        name="squares",
    )(*(pin(x) for x in parts))

    col_sum = sum_over_devices(col_sum)
    scale = 1.0 / (col_sum * (1.0 / (n_row * IB * block)) + 1e-06)
    return (sq * scale)[None]


def solution(mesh):
    return jax.shard_map(
        body,
        mesh=mesh,
        in_specs=(
            P(("layer", "row", "col"), None, None, None),
            P(("layer", "row", "col"), None),
            P(("layer", "row", "col")),
            P(("layer", "row"), "col"),
        ),
        out_specs=P("row", "layer", "col"),
        check_vma=False,
    )
```

```python
import functools

import jax
import jax.numpy as jnp
import numpy as np
from jax import lax
from jax.experimental import pallas as pl
from jax.experimental.pallas import tpu as pltpu
from jax.sharding import PartitionSpec as P

IB = 16
AXES = ("layer", "row", "col")
BITS, VALUES, WORDS = 18, 16, 9
VMEM = pl.BlockSpec(memory_space=pltpu.VMEM)


def pin(x):
    return pltpu.with_memory_space_constraint(x, pltpu.VMEM)


def xor_permute(x, axis, mask):
    return lax.ppermute(x, axis, [(i, i ^ mask) for i in range(lax.axis_size(axis))])


def grid_permute(x, masks, other_masks=None):
    sizes = [lax.axis_size(a) for a in AXES]
    pairs = []
    for source, at in enumerate(np.ndindex(*sizes)):
        by = other_masks if other_masks and at[0] % 2 else masks
        target = [i ^ m for i, m in zip(at, by, strict=True)]
        pairs.append((source, int(np.ravel_multi_index(target, sizes))))
    return lax.ppermute(x, AXES, pairs)


def sum_over_devices(x):
    n_layer, n_row, _ = (lax.axis_size(a) for a in AXES)
    chips = [(i, j, 0) for i in range(0, n_layer, 2) for j in range(n_row)][:0:-1]
    got = [grid_permute(x, chips.pop(0))] if len(chips) % 2 else []
    x = x + xor_permute(x, "layer", 1)
    got += [grid_permute(x, *chips[k : k + 2]) for k in range(0, len(chips), 2)]
    got = sum(got)
    return x + (got + xor_permute(got, "layer", 1))


def power_of_two(k):
    scale = jnp.ones(k.shape, jnp.float32)
    for b in range(7):
        factor = jnp.where(k < 0, 2.0 ** -(2**b), 2.0 ** (2**b))
        scale = jnp.where((jnp.abs(k) >> b) & 1 == 1, scale * factor, scale)
    return scale


def low_fields(i):
    fields, at, bit = [], (i - WORDS) * BITS, 0
    while bit < BITS:
        word, to = divmod(at, 32 - BITS)
        bits = min(BITS - bit, 32 - BITS - to)
        fields.append((bit, word, to, bits))
        at, bit = at + bits, bit + bits
    return fields


def pack(part, out_ref):
    top = jnp.max(jnp.abs(part), axis=0, keepdims=True)
    k = jnp.clip(jnp.ceil(jnp.log2(top) + 0.01), -100.0, 126.0).astype(jnp.int32)
    q = jnp.floor(part * power_of_two(BITS - 1 - k) + 0.5).astype(jnp.int32)
    rows = part.shape[0] // VALUES
    q = [q[i * rows : (i + 1) * rows] for i in range(VALUES)]
    words = [q[j] << (32 - BITS) for j in range(WORDS)]
    for i in range(WORDS, VALUES):
        for bit, word, to, bits in low_fields(i):
            words[word] = words[word] | (((q[i] >> bit) & ((1 << bits) - 1)) << to)
    for j in range(WORDS):
        out_ref[j * rows : (j + 1) * rows] = words[j]
    out_ref[WORDS * rows :] = jnp.broadcast_to(k, (8, part.shape[1]))


def unpack(ref, rows, i):
    if i < WORDS:
        return ref[i * rows : (i + 1) * rows] >> (32 - BITS)
    total = None
    for bit, word, to, bits in low_fields(i):
        w = ref[word * rows : (word + 1) * rows]
        if bit + bits == BITS:
            w = ((w << (32 - to - bits)) >> (32 - bits)) << bit
        else:
            w = ((w >> to) & ((1 << bits) - 1)) << bit
        total = w if total is None else total | w
    return total


def square_kernel(mine_ref, *refs):
    coded_refs, (sq_ref, sum_ref) = refs[:-2], refs[-2:]
    rows = mine_ref.shape[0] // VALUES
    scales = [power_of_two(ref[WORDS * rows : WORDS * rows + 1] - (BITS - 1)) for ref in coded_refs]
    total = jnp.zeros(sum_ref.shape, jnp.float32)
    for i in range(VALUES):
        at = slice(i * rows, (i + 1) * rows)
        e = mine_ref[at]
        for ref, scale in zip(coded_refs, scales):
            e = e + unpack(ref, rows, i).astype(jnp.float32) * scale
        sq = e * e
        sq_ref[at] = sq
        total = total + jnp.sum(sq, axis=0, keepdims=True)
    sum_ref[...] = total


def places(lists):
    place = lax.broadcasted_iota(jnp.int32, lists.shape, 1)
    bits = (place ^ 8) << ((lists & 7) * 4)
    none = sum(8 << (4 * i) for i in range(8)) - (1 << 32)
    words = [
        jnp.sum(jnp.where(lists >> 3 == h, bits, 0), axis=1, keepdims=True) ^ none
        for h in range(IB // 8)
    ]
    return [[word[k, 0] for word in words] for k in range(lists.shape[0])]


def product_kernel(masks, n_layer, n_row, n_col, lists_ref, *refs):
    n_slots, n_held = n_layer // 2, 2 * len(masks)
    mine_refs, near_refs = refs[:2], refs[2 : 2 + 2 * n_row]
    a_refs, out_refs = refs[2 + 2 * n_row : 2 + 2 * n_row + n_held], refs[2 + 2 * n_row + n_held : -1]
    lhs_ref = refs[-1]
    layer, row, col = (lax.axis_index(n) for n in ("layer", "row", "col"))
    per, per_row = IB // n_layer, n_col // n_row
    capacity, block, depth = a_refs[0].shape
    lists = places(lists_ref[...])
    rhs = []
    for k in range(n_held):
        other, place = k % 2, k // 2
        panel = col ^ masks[place]
        at = panel % per_row * depth
        owner = (panel // per_row) ^ row
        start = pl.multiple_of(owner * (per_row * depth) + at, depth)
        mine = mine_refs[other][pl.ds(start, depth), :]
        at = pl.ds(pl.multiple_of(at, depth), depth)
        near = near_refs[other][at, :]
        for i in range(1, n_row):
            near = jnp.where(owner == i, near_refs[2 * i + other][at, :], near)
        rhs.append(jnp.concatenate([mine, near], axis=1))
    rhs = jnp.concatenate(rhs, axis=0)
    width, parts = rhs.shape[1] // 2, []
    for slot in range(n_slots):
        for sub in range(per):
            block_row = (layer ^ (2 * slot)) * per + sub
            for k in range(n_held):
                word = lists[k][0]
                for h in range(1, len(lists[k])):
                    word = jnp.where(block_row // 8 == h, lists[k][h], word)
                n = (word >> (block_row % 8 * 4)) & 15
                a = a_refs[k][jnp.minimum(n, capacity - 1)]
                lhs_ref[slot, sub * block : (sub + 1) * block, k * depth : (k + 1) * depth] = (
                    jnp.where(n < capacity, a, jnp.zeros_like(a))
                )
        out = jnp.dot(lhs_ref[slot], rhs, preferred_element_type=jnp.float32)
        parts += [out[:, m * width : (m + 1) * width] for m in range(2)]
    out_refs[0][...] = parts[0]
    for k in range(1, 2 * n_slots - 1, 2):
        one, two = parts[k : k + 2]
        pack(jnp.where(layer % 2 == 0, one, two), out_refs[k])
        pack(jnp.where(layer % 2 == 0, two, one), out_refs[k + 1])
    pack(parts[-1], out_refs[-1])


def products(masks, lists, b_refs, panels):
    n_layer, n_row, n_col = (lax.axis_size(a) for a in ("layer", "row", "col"))
    _, block, depth = panels[0].shape
    rows, n_slots, width = IB // n_layer * block, n_layer // 2, b_refs[0].shape[1]
    ins = [lists, *b_refs, *panels]
    return pl.pallas_call(
        functools.partial(product_kernel, masks, n_layer, n_row, n_col),
        out_shape=[pltpu.VMEM((rows, width), jnp.float32)]
        + [pltpu.VMEM((rows // VALUES * WORDS + 8, width), jnp.int32)] * (2 * n_slots - 1),
        in_specs=[VMEM] * len(ins),
        out_specs=[VMEM] * (2 * n_slots),
        scratch_shapes=[
            pltpu.VMEM((n_slots, rows, len(panels) * depth), jnp.bfloat16),
        ],
        name="partial_rows",
    )(*(pin(x) for x in ins))


def body(a_blocks, a_rows, a_count, b_panel):
    n_layer, n_row, n_col = (lax.axis_size(a) for a in ("layer", "row", "col"))
    _, capacity, block, _ = a_blocks.shape

    def other(x):
        return xor_permute(x, "layer", 1)

    masks, panels = [0], [a_blocks[0]]
    valid = jnp.arange(capacity, dtype=jnp.int32)[None, :] < a_count[:, None]
    lists = jnp.where(valid, a_rows, IB)
    lists = jnp.concatenate([lists, other(lists)])
    bit = n_col // 2
    while bit > 1:
        panels = panels + [xor_permute(p, "col", bit) for p in panels]
        lists = jnp.concatenate([lists, xor_permute(lists, "col", bit)])
        masks = masks + [m ^ bit for m in masks]
        bit //= 2

    own_other = other(panels[0])
    b_panel, own_other = lax.optimization_barrier((b_panel, own_other))

    b_rows = [[b_panel, xor_permute(b_panel, "col", 1)]]
    bit = 1
    while bit < n_row:
        b_rows = b_rows + [[xor_permute(b, "row", bit) for b in pair] for pair in b_rows]
        bit *= 2

    mine = jnp.concatenate([pair[0] for pair in b_rows])
    mine = [mine, other(mine)]
    near = [pair[1] for pair in b_rows]
    own = a_blocks[0]
    far, lists, mine, near, own_other = lax.optimization_barrier(
        (panels[1:], lists, mine, near, own_other)
    )
    near = [x for b in near for x in (b, other(b))]
    panels = [own, own_other] + [x for p in far for x in (p, other(p))]
    b_refs = mine + near
    parts = products(masks, lists, b_refs, panels)

    masks = [(2 * (k // 2), 0, k % 2) for k in range(n_layer)]
    swaps = [0] + [k + 1 if k % 2 else k - 1 for k in range(1, n_layer - 1)] + [n_layer - 1]
    parts = [parts[0]] + [
        grid_permute(parts[k], masks[k], masks[swaps[k]]) for k in range(1, n_layer)
    ]
    sq, col_sum = pl.pallas_call(
        square_kernel,
        out_shape=(
            pltpu.VMEM(parts[0].shape, jnp.float32),
            pltpu.VMEM((1, parts[0].shape[1]), jnp.float32),
        ),
        in_specs=[VMEM] * len(parts),
        out_specs=(VMEM, VMEM),
        name="squares",
    )(*(pin(x) for x in parts))

    col_sum = sum_over_devices(col_sum)
    scale = 1.0 / (col_sum * (1.0 / (n_row * IB * block)) + 1e-06)
    return (sq * scale)[None]


def solution(mesh):
    return jax.shard_map(
        body,
        mesh=mesh,
        in_specs=(
            P(("layer", "row", "col"), None, None, None),
            P(("layer", "row", "col"), None),
            P(("layer", "row", "col")),
            P(("layer", "row"), "col"),
        ),
        out_specs=P("row", "layer", "col"),
        check_vma=False,
    )
```

```python
import functools

import jax
import jax.numpy as jnp
import numpy as np
from jax import lax
from jax.experimental import pallas as pl
from jax.experimental.pallas import tpu as pltpu
from jax.sharding import PartitionSpec as P

IB = 16
AXES = ("layer", "row", "col")
BITS, VALUES, WORDS = 18, 16, 9
VMEM = pl.BlockSpec(memory_space=pltpu.VMEM)


def pin(x):
    return pltpu.with_memory_space_constraint(x, pltpu.VMEM)


def xor_permute(x, axis, mask):
    return lax.ppermute(x, axis, [(i, i ^ mask) for i in range(lax.axis_size(axis))])


def grid_permute(x, masks, other_masks=None):
    sizes = [lax.axis_size(a) for a in AXES]
    pairs = []
    for source, at in enumerate(np.ndindex(*sizes)):
        by = other_masks if other_masks and at[0] % 2 else masks
        target = [i ^ m for i, m in zip(at, by, strict=True)]
        pairs.append((source, int(np.ravel_multi_index(target, sizes))))
    return lax.ppermute(x, AXES, pairs)


def sum_over_devices(x):
    n_layer, n_row, _ = (lax.axis_size(a) for a in AXES)
    chips = [(i, j, 0) for i in range(0, n_layer, 2) for j in range(n_row)][:0:-1]
    got = [grid_permute(x, chips.pop(0))] if len(chips) % 2 else []
    x = x + xor_permute(x, "layer", 1)
    got += [grid_permute(x, *chips[k : k + 2]) for k in range(0, len(chips), 2)]
    got = sum(got)
    return x + (got + xor_permute(got, "layer", 1))


def power_of_two(k):
    scale = jnp.ones(k.shape, jnp.float32)
    for b in range(7):
        factor = jnp.where(k < 0, 2.0 ** -(2**b), 2.0 ** (2**b))
        scale = jnp.where((jnp.abs(k) >> b) & 1 == 1, scale * factor, scale)
    return scale


def low_fields(i):
    fields, at, bit = [], (i - WORDS) * BITS, 0
    while bit < BITS:
        word, to = divmod(at, 32 - BITS)
        bits = min(BITS - bit, 32 - BITS - to)
        fields.append((bit, word, to, bits))
        at, bit = at + bits, bit + bits
    return fields


def pack(parts, out_refs):
    top = jnp.concatenate([jnp.max(jnp.abs(p), axis=0, keepdims=True) for p in parts])
    k = jnp.clip(jnp.ceil(jnp.log2(top) + 0.01), -100.0, 126.0).astype(jnp.int32)
    steps = power_of_two(BITS - 1 - k)
    for p, (part, out_ref) in enumerate(zip(parts, out_refs, strict=True)):
        q = jnp.floor(part * steps[p : p + 1] + 0.5).astype(jnp.int32)
        rows = part.shape[0] // VALUES
        q = [q[i * rows : (i + 1) * rows] for i in range(VALUES)]
        words = [q[j] << (32 - BITS) for j in range(WORDS)]
        for i in range(WORDS, VALUES):
            for bit, word, to, bits in low_fields(i):
                words[word] = words[word] | (((q[i] >> bit) & ((1 << bits) - 1)) << to)
        for j in range(WORDS):
            out_ref[j * rows : (j + 1) * rows] = words[j]
        out_ref[WORDS * rows :] = jnp.broadcast_to(k[p : p + 1], (8, part.shape[1]))


def unpack(ref, rows, i):
    if i < WORDS:
        return ref[i * rows : (i + 1) * rows] >> (32 - BITS)
    total = None
    for bit, word, to, bits in low_fields(i):
        w = ref[word * rows : (word + 1) * rows]
        if bit + bits == BITS:
            w = ((w << (32 - to - bits)) >> (32 - bits)) << bit
        else:
            w = ((w >> to) & ((1 << bits) - 1)) << bit
        total = w if total is None else total | w
    return total


def square_kernel(mine_ref, *refs):
    coded_refs, (sq_ref, sum_ref) = refs[:-2], refs[-2:]
    rows = mine_ref.shape[0] // VALUES
    scales = [power_of_two(ref[WORDS * rows : WORDS * rows + 1] - (BITS - 1)) for ref in coded_refs]
    total = jnp.zeros(sum_ref.shape, jnp.float32)
    for i in range(VALUES):
        at = slice(i * rows, (i + 1) * rows)
        e = mine_ref[at]
        for ref, scale in zip(coded_refs, scales):
            e = e + unpack(ref, rows, i).astype(jnp.float32) * scale
        sq = e * e
        sq_ref[at] = sq
        total = total + jnp.sum(sq, axis=0, keepdims=True)
    sum_ref[...] = total


def places(lists):
    place = lax.broadcasted_iota(jnp.int32, lists.shape, 1)
    bits = (place ^ 8) << ((lists & 7) * 4)
    none = sum(8 << (4 * i) for i in range(8)) - (1 << 32)
    words = [
        jnp.sum(jnp.where(lists >> 3 == h, bits, 0), axis=1, keepdims=True) ^ none
        for h in range(IB // 8)
    ]
    return [[word[k, 0] for word in words] for k in range(lists.shape[0])]


def product_kernel(masks, n_layer, n_row, n_col, lists_ref, *refs):
    n_slots, n_held = n_layer // 2, 2 * len(masks)
    mine_refs, near_refs = refs[:2], refs[2 : 2 + 2 * n_row]
    a_refs, out_refs = refs[2 + 2 * n_row : 2 + 2 * n_row + n_held], refs[2 + 2 * n_row + n_held : -1]
    lhs_ref = refs[-1]
    layer, row, col = (lax.axis_index(n) for n in ("layer", "row", "col"))
    per, per_row = IB // n_layer, n_col // n_row
    capacity, block, depth = a_refs[0].shape
    lists = places(lists_ref[...])
    rhs = []
    for k in range(n_held):
        other, place = k % 2, k // 2
        panel = col ^ masks[place]
        at = panel % per_row * depth
        owner = (panel // per_row) ^ row
        start = pl.multiple_of(owner * (per_row * depth) + at, depth)
        mine = mine_refs[other][pl.ds(start, depth), :]
        at = pl.ds(pl.multiple_of(at, depth), depth)
        near = near_refs[other][at, :]
        for i in range(1, n_row):
            near = jnp.where(owner == i, near_refs[2 * i + other][at, :], near)
        rhs.append(jnp.concatenate([mine, near], axis=1))
    rhs = jnp.concatenate(rhs, axis=0)
    width, parts = rhs.shape[1] // 2, []
    for slot in range(n_slots):
        for sub in range(per):
            block_row = (layer ^ (2 * slot)) * per + sub
            for k in range(n_held):
                word = lists[k][0]
                for h in range(1, len(lists[k])):
                    word = jnp.where(block_row // 8 == h, lists[k][h], word)
                n = (word >> (block_row % 8 * 4)) & 15
                a = a_refs[k][jnp.minimum(n, capacity - 1)]
                lhs_ref[slot, sub * block : (sub + 1) * block, k * depth : (k + 1) * depth] = (
                    jnp.where(n < capacity, a, jnp.zeros_like(a))
                )
        out = jnp.dot(lhs_ref[slot], rhs, preferred_element_type=jnp.float32)
        parts += [out[:, m * width : (m + 1) * width] for m in range(2)]
    out_refs[0][...] = parts[0]
    for k in range(1, 2 * n_slots - 1, 2):
        one, two = parts[k : k + 2]
        parts[k] = jnp.where(layer % 2 == 0, one, two)
        parts[k + 1] = jnp.where(layer % 2 == 0, two, one)
    pack(parts[1:], out_refs[1:])


def products(masks, lists, b_refs, panels):
    n_layer, n_row, n_col = (lax.axis_size(a) for a in ("layer", "row", "col"))
    _, block, depth = panels[0].shape
    rows, n_slots, width = IB // n_layer * block, n_layer // 2, b_refs[0].shape[1]
    ins = [lists, *b_refs, *panels]
    return pl.pallas_call(
        functools.partial(product_kernel, masks, n_layer, n_row, n_col),
        out_shape=[pltpu.VMEM((rows, width), jnp.float32)]
        + [pltpu.VMEM((rows // VALUES * WORDS + 8, width), jnp.int32)] * (2 * n_slots - 1),
        in_specs=[VMEM] * len(ins),
        out_specs=[VMEM] * (2 * n_slots),
        scratch_shapes=[
            pltpu.VMEM((n_slots, rows, len(panels) * depth), jnp.bfloat16),
        ],
        name="partial_rows",
    )(*(pin(x) for x in ins))


def body(a_blocks, a_rows, a_count, b_panel):
    n_layer, n_row, n_col = (lax.axis_size(a) for a in ("layer", "row", "col"))
    _, capacity, block, _ = a_blocks.shape

    def other(x):
        return xor_permute(x, "layer", 1)

    masks, panels = [0], [a_blocks[0]]
    valid = jnp.arange(capacity, dtype=jnp.int32)[None, :] < a_count[:, None]
    lists = jnp.where(valid, a_rows, IB)
    lists = jnp.concatenate([lists, other(lists)])
    bit = n_col // 2
    while bit > 1:
        panels = panels + [xor_permute(p, "col", bit) for p in panels]
        lists = jnp.concatenate([lists, xor_permute(lists, "col", bit)])
        masks = masks + [m ^ bit for m in masks]
        bit //= 2

    own_other = other(panels[0])
    b_panel, own_other = lax.optimization_barrier((b_panel, own_other))

    b_rows = [[b_panel, xor_permute(b_panel, "col", 1)]]
    bit = 1
    while bit < n_row:
        b_rows = b_rows + [[xor_permute(b, "row", bit) for b in pair] for pair in b_rows]
        bit *= 2

    mine = jnp.concatenate([pair[0] for pair in b_rows])
    mine = [mine, other(mine)]
    near = [pair[1] for pair in b_rows]
    own = a_blocks[0]
    far, lists, mine, near, own_other = lax.optimization_barrier(
        (panels[1:], lists, mine, near, own_other)
    )
    near = [x for b in near for x in (b, other(b))]
    panels = [own, own_other] + [x for p in far for x in (p, other(p))]
    b_refs = mine + near
    parts = products(masks, lists, b_refs, panels)

    masks = [(2 * (k // 2), 0, k % 2) for k in range(n_layer)]
    swaps = [0] + [k + 1 if k % 2 else k - 1 for k in range(1, n_layer - 1)] + [n_layer - 1]
    parts = [parts[0]] + [
        grid_permute(parts[k], masks[k], masks[swaps[k]]) for k in range(1, n_layer)
    ]
    sq, col_sum = pl.pallas_call(
        square_kernel,
        out_shape=(
            pltpu.VMEM(parts[0].shape, jnp.float32),
            pltpu.VMEM((1, parts[0].shape[1]), jnp.float32),
        ),
        in_specs=[VMEM] * len(parts),
        out_specs=(VMEM, VMEM),
        name="squares",
    )(*(pin(x) for x in parts))

    col_sum = sum_over_devices(col_sum)
    scale = 1.0 / (col_sum * (1.0 / (n_row * IB * block)) + 1e-06)
    return (sq * scale)[None]


def solution(mesh):
    return jax.shard_map(
        body,
        mesh=mesh,
        in_specs=(
            P(("layer", "row", "col"), None, None, None),
            P(("layer", "row", "col"), None),
            P(("layer", "row", "col")),
            P(("layer", "row"), "col"),
        ),
        out_specs=P("row", "layer", "col"),
        check_vma=False,
    )
```

```python
import functools

import jax
import jax.numpy as jnp
import numpy as np
from jax import lax
from jax.experimental import pallas as pl
from jax.experimental.pallas import tpu as pltpu
from jax.sharding import PartitionSpec as P

IB = 16
AXES = ("layer", "row", "col")
BITS, VALUES, WORDS = 18, 16, 9
VMEM = pl.BlockSpec(memory_space=pltpu.VMEM)


def pin(x):
    return pltpu.with_memory_space_constraint(x, pltpu.VMEM)


def xor_permute(x, axis, mask):
    return lax.ppermute(x, axis, [(i, i ^ mask) for i in range(lax.axis_size(axis))])


def grid_permute(x, masks, other_masks=None):
    sizes = [lax.axis_size(a) for a in AXES]
    pairs = []
    for source, at in enumerate(np.ndindex(*sizes)):
        by = other_masks if other_masks and at[0] % 2 else masks
        target = [i ^ m for i, m in zip(at, by, strict=True)]
        pairs.append((source, int(np.ravel_multi_index(target, sizes))))
    return lax.ppermute(x, AXES, pairs)


def sum_over_devices(x):
    n_layer, n_row, _ = (lax.axis_size(a) for a in AXES)
    chips = [(i, j, 0) for i in range(0, n_layer, 2) for j in range(n_row)][:0:-1]
    got = [grid_permute(x, chips.pop(0))] if len(chips) % 2 else []
    x = x + xor_permute(x, "layer", 1)
    got += [grid_permute(x, *chips[k : k + 2]) for k in range(0, len(chips), 2)]
    got = sum(got)
    return x + (got + xor_permute(got, "layer", 1))


def power_of_two(k):
    scale = jnp.ones(k.shape, jnp.float32)
    for b in range(7):
        factor = jnp.where(k < 0, 2.0 ** -(2**b), 2.0 ** (2**b))
        scale = jnp.where((jnp.abs(k) >> b) & 1 == 1, scale * factor, scale)
    return scale


def low_fields(i):
    fields, at, bit = [], (i - WORDS) * BITS, 0
    while bit < BITS:
        word, to = divmod(at, 32 - BITS)
        bits = min(BITS - bit, 32 - BITS - to)
        fields.append((bit, word, to, bits))
        at, bit = at + bits, bit + bits
    return fields


def pack(parts, out_refs):
    top = jnp.concatenate([jnp.max(jnp.abs(p), axis=0, keepdims=True) for p in parts])
    k = jnp.clip(jnp.ceil(jnp.log2(top) + 0.01), -100.0, 126.0).astype(jnp.int32)
    steps = power_of_two(BITS - 1 - k)
    for p, (part, out_ref) in enumerate(zip(parts, out_refs, strict=True)):
        q = jnp.floor(part * steps[p : p + 1] + 0.5).astype(jnp.int32)
        rows = part.shape[0] // VALUES
        q = [q[i * rows : (i + 1) * rows] for i in range(VALUES)]
        words = [q[j] << (32 - BITS) for j in range(WORDS)]
        for i in range(WORDS, VALUES):
            for bit, word, to, bits in low_fields(i):
                words[word] = words[word] | (((q[i] >> bit) & ((1 << bits) - 1)) << to)
        for j in range(WORDS):
            out_ref[j * rows : (j + 1) * rows] = words[j]
        out_ref[WORDS * rows :] = jnp.broadcast_to(k[p : p + 1], (8, part.shape[1]))


def unpack(ref, rows, i):
    if i < WORDS:
        return ref[i * rows : (i + 1) * rows] >> (32 - BITS)
    total = None
    for bit, word, to, bits in low_fields(i):
        w = ref[word * rows : (word + 1) * rows]
        if bit + bits == BITS:
            w = ((w << (32 - to - bits)) >> (32 - bits)) << bit
        else:
            w = ((w >> to) & ((1 << bits) - 1)) << bit
        total = w if total is None else total | w
    return total


def square_kernel(mine_ref, *refs):
    coded_refs, (sq_ref, sum_ref) = refs[:-2], refs[-2:]
    rows = mine_ref.shape[0] // VALUES
    scales = [power_of_two(ref[WORDS * rows : WORDS * rows + 1] - (BITS - 1)) for ref in coded_refs]
    total = jnp.zeros(sum_ref.shape, jnp.float32)
    for i in range(VALUES):
        at = slice(i * rows, (i + 1) * rows)
        e = mine_ref[at]
        for ref, scale in zip(coded_refs, scales):
            e = e + unpack(ref, rows, i).astype(jnp.float32) * scale
        sq = e * e
        sq_ref[at] = sq
        total = total + jnp.sum(sq, axis=0, keepdims=True)
    sum_ref[...] = total


def places(lists):
    place = lax.broadcasted_iota(jnp.int32, lists.shape, 1)
    bits = (place ^ 8) << ((lists & 7) * 4)
    none = sum(8 << (4 * i) for i in range(8)) - (1 << 32)
    words = [
        jnp.sum(jnp.where(lists >> 3 == h, bits, 0), axis=1, keepdims=True) ^ none
        for h in range(IB // 8)
    ]
    return [[word[k, 0] for word in words] for k in range(lists.shape[0])]


def scale_kernel(share, sq_ref, sum_ref, out_ref, held_ref, sems):
    scale = 1.0 / (sum_ref[...] * share + 1e-06)
    half, copies = sq_ref.shape[0] // 2, []
    for i in range(2):
        at = pl.ds(i * half, half)
        held_ref[at, :] = sq_ref[at, :] * scale
        copies.append(pltpu.make_async_copy(held_ref.at[at], out_ref.at[at], sems.at[i]))
        copies[i].start()
    for copy in copies:
        copy.wait()


def product_kernel(masks, n_layer, n_row, n_col, lists_ref, *refs):
    n_slots, n_held = n_layer // 2, 2 * len(masks)
    mine_refs, near_refs = refs[:2], refs[2 : 2 + 2 * n_row]
    a_refs, out_refs = refs[2 + 2 * n_row : 2 + 2 * n_row + n_held], refs[2 + 2 * n_row + n_held : -1]
    lhs_ref = refs[-1]
    layer, row, col = (lax.axis_index(n) for n in ("layer", "row", "col"))
    per, per_row = IB // n_layer, n_col // n_row
    capacity, block, depth = a_refs[0].shape
    lists = places(lists_ref[...])
    rhs = []
    for k in range(n_held):
        other, place = k % 2, k // 2
        panel = col ^ masks[place]
        at = panel % per_row * depth
        owner = (panel // per_row) ^ row
        start = pl.multiple_of(owner * (per_row * depth) + at, depth)
        mine = mine_refs[other][pl.ds(start, depth), :]
        at = pl.ds(pl.multiple_of(at, depth), depth)
        near = near_refs[other][at, :]
        for i in range(1, n_row):
            near = jnp.where(owner == i, near_refs[2 * i + other][at, :], near)
        rhs.append(jnp.concatenate([mine, near], axis=1))
    rhs = jnp.concatenate(rhs, axis=0)
    width, parts = rhs.shape[1] // 2, []
    for slot in range(n_slots):
        for sub in range(per):
            block_row = (layer ^ (2 * slot)) * per + sub
            for k in range(n_held):
                word = lists[k][0]
                for h in range(1, len(lists[k])):
                    word = jnp.where(block_row // 8 == h, lists[k][h], word)
                n = (word >> (block_row % 8 * 4)) & 15
                a = a_refs[k][jnp.minimum(n, capacity - 1)]
                lhs_ref[slot, sub * block : (sub + 1) * block, k * depth : (k + 1) * depth] = (
                    jnp.where(n < capacity, a, jnp.zeros_like(a))
                )
        out = jnp.dot(lhs_ref[slot], rhs, preferred_element_type=jnp.float32)
        parts += [out[:, m * width : (m + 1) * width] for m in range(2)]
    out_refs[0][...] = parts[0]
    for k in range(1, 2 * n_slots - 1, 2):
        one, two = parts[k : k + 2]
        parts[k] = jnp.where(layer % 2 == 0, one, two)
        parts[k + 1] = jnp.where(layer % 2 == 0, two, one)
    pack(parts[1:], out_refs[1:])


def products(masks, lists, b_refs, panels):
    n_layer, n_row, n_col = (lax.axis_size(a) for a in ("layer", "row", "col"))
    _, block, depth = panels[0].shape
    rows, n_slots, width = IB // n_layer * block, n_layer // 2, b_refs[0].shape[1]
    ins = [lists, *b_refs, *panels]
    return pl.pallas_call(
        functools.partial(product_kernel, masks, n_layer, n_row, n_col),
        out_shape=[pltpu.VMEM((rows, width), jnp.float32)]
        + [pltpu.VMEM((rows // VALUES * WORDS + 8, width), jnp.int32)] * (2 * n_slots - 1),
        in_specs=[VMEM] * len(ins),
        out_specs=[VMEM] * (2 * n_slots),
        scratch_shapes=[
            pltpu.VMEM((n_slots, rows, len(panels) * depth), jnp.bfloat16),
        ],
        name="partial_rows",
    )(*(pin(x) for x in ins))


def body(a_blocks, a_rows, a_count, b_panel):
    n_layer, n_row, n_col = (lax.axis_size(a) for a in ("layer", "row", "col"))
    _, capacity, block, _ = a_blocks.shape

    def other(x):
        return xor_permute(x, "layer", 1)

    masks, panels = [0], [a_blocks[0]]
    valid = jnp.arange(capacity, dtype=jnp.int32)[None, :] < a_count[:, None]
    lists = jnp.where(valid, a_rows, IB)
    lists = jnp.concatenate([lists, other(lists)])
    bit = n_col // 2
    while bit > 1:
        panels = panels + [xor_permute(p, "col", bit) for p in panels]
        lists = jnp.concatenate([lists, xor_permute(lists, "col", bit)])
        masks = masks + [m ^ bit for m in masks]
        bit //= 2

    own_other = other(panels[0])
    b_panel, own_other = lax.optimization_barrier((b_panel, own_other))

    b_rows = [[b_panel, xor_permute(b_panel, "col", 1)]]
    bit = 1
    while bit < n_row:
        b_rows = b_rows + [[xor_permute(b, "row", bit) for b in pair] for pair in b_rows]
        bit *= 2

    mine = jnp.concatenate([pair[0] for pair in b_rows])
    mine = [mine, other(mine)]
    near = [pair[1] for pair in b_rows]
    own = a_blocks[0]
    far, lists, mine, near, own_other = lax.optimization_barrier(
        (panels[1:], lists, mine, near, own_other)
    )
    near = [x for b in near for x in (b, other(b))]
    panels = [own, own_other] + [x for p in far for x in (p, other(p))]
    b_refs = mine + near
    parts = products(masks, lists, b_refs, panels)

    masks = [(2 * (k // 2), 0, k % 2) for k in range(n_layer)]
    swaps = [0] + [k + 1 if k % 2 else k - 1 for k in range(1, n_layer - 1)] + [n_layer - 1]
    parts = [parts[0]] + [
        grid_permute(parts[k], masks[k], masks[swaps[k]]) for k in range(1, n_layer)
    ]
    sq, col_sum = pl.pallas_call(
        square_kernel,
        out_shape=(
            pltpu.VMEM(parts[0].shape, jnp.float32),
            pltpu.VMEM((1, parts[0].shape[1]), jnp.float32),
        ),
        in_specs=[VMEM] * len(parts),
        out_specs=(VMEM, VMEM),
        name="squares",
    )(*(pin(x) for x in parts))

    col_sum = sum_over_devices(col_sum)
    flow = pl.pallas_call(
        functools.partial(scale_kernel, 1.0 / (n_row * IB * block)),
        out_shape=jax.ShapeDtypeStruct(sq.shape, jnp.float32),
        in_specs=[VMEM] * 2,
        out_specs=pl.BlockSpec(memory_space=pl.ANY),
        scratch_shapes=[pltpu.VMEM(sq.shape, jnp.float32), pltpu.SemaphoreType.DMA((2,))],
        name="scale",
    )(pin(sq), pin(col_sum))
    return flow[None]


def solution(mesh):
    return jax.shard_map(
        body,
        mesh=mesh,
        in_specs=(
            P(("layer", "row", "col"), None, None, None),
            P(("layer", "row", "col"), None),
            P(("layer", "row", "col")),
            P(("layer", "row"), "col"),
        ),
        out_specs=P("row", "layer", "col"),
        check_vma=False,
    )
```

```python
import functools

import jax
import jax.numpy as jnp
import numpy as np
from jax import lax
from jax.experimental import pallas as pl
from jax.experimental.pallas import tpu as pltpu
from jax.sharding import PartitionSpec as P

IB = 16
AXES = ("layer", "row", "col")
BITS, VALUES, WORDS = 18, 16, 9
VMEM = pl.BlockSpec(memory_space=pltpu.VMEM)


def pin(x):
    return pltpu.with_memory_space_constraint(x, pltpu.VMEM)


def xor_permute(x, axis, mask):
    return lax.ppermute(x, axis, [(i, i ^ mask) for i in range(lax.axis_size(axis))])


def grid_permute(x, masks, other_masks=None):
    sizes = [lax.axis_size(a) for a in AXES]
    pairs = []
    for source, at in enumerate(np.ndindex(*sizes)):
        by = other_masks if other_masks and at[0] % 2 else masks
        target = [i ^ m for i, m in zip(at, by, strict=True)]
        pairs.append((source, int(np.ravel_multi_index(target, sizes))))
    return lax.ppermute(x, AXES, pairs)


def sum_over_devices(x):
    n_layer, n_row, _ = (lax.axis_size(a) for a in AXES)
    chips = [(i, j, 0) for i in range(0, n_layer, 2) for j in range(n_row)][:0:-1]
    got = [grid_permute(x, chips.pop(0))] if len(chips) % 2 else []
    x = x + xor_permute(x, "layer", 1)
    got += [grid_permute(x, *chips[k : k + 2]) for k in range(0, len(chips), 2)]
    got = sum(got)
    return x + (got + xor_permute(got, "layer", 1))


def power_of_two(k):
    scale = jnp.ones(k.shape, jnp.float32)
    for b in range(7):
        factor = jnp.where(k < 0, 2.0 ** -(2**b), 2.0 ** (2**b))
        scale = jnp.where((jnp.abs(k) >> b) & 1 == 1, scale * factor, scale)
    return scale


def low_fields(i):
    fields, at, bit = [], (i - WORDS) * BITS, 0
    while bit < BITS:
        word, to = divmod(at, 32 - BITS)
        bits = min(BITS - bit, 32 - BITS - to)
        fields.append((bit, word, to, bits))
        at, bit = at + bits, bit + bits
    return fields


def pack(parts, out_refs):
    top = jnp.concatenate([jnp.max(jnp.abs(p), axis=0, keepdims=True) for p in parts])
    k = jnp.clip(jnp.ceil(jnp.log2(top) + 0.01), -100.0, 126.0).astype(jnp.int32)
    steps = power_of_two(BITS - 1 - k)
    for p, (part, out_ref) in enumerate(zip(parts, out_refs, strict=True)):
        q = jnp.floor(part * steps[p : p + 1] + 0.5).astype(jnp.int32)
        rows = part.shape[0] // VALUES
        q = [q[i * rows : (i + 1) * rows] for i in range(VALUES)]
        words = [q[j] << (32 - BITS) for j in range(WORDS)]
        for i in range(WORDS, VALUES):
            for bit, word, to, bits in low_fields(i):
                words[word] = words[word] | (((q[i] >> bit) & ((1 << bits) - 1)) << to)
        for j in range(WORDS):
            out_ref[j * rows : (j + 1) * rows] = words[j]
        out_ref[WORDS * rows :] = jnp.broadcast_to(k[p : p + 1], (8, part.shape[1]))


def unpack(ref, rows, i):
    if i < WORDS:
        return ref[i * rows : (i + 1) * rows] >> (32 - BITS)
    total = None
    for bit, word, to, bits in low_fields(i):
        w = ref[word * rows : (word + 1) * rows]
        if bit + bits == BITS:
            w = ((w << (32 - to - bits)) >> (32 - bits)) << bit
        else:
            w = ((w >> to) & ((1 << bits) - 1)) << bit
        total = w if total is None else total | w
    return total


def square_kernel(mine_ref, *refs):
    coded_refs, (sq_ref, sum_ref) = refs[:-2], refs[-2:]
    rows = mine_ref.shape[0] // VALUES
    scales = [power_of_two(ref[WORDS * rows : WORDS * rows + 1] - (BITS - 1)) for ref in coded_refs]
    total = jnp.zeros(sum_ref.shape, jnp.float32)
    for i in range(VALUES):
        at = slice(i * rows, (i + 1) * rows)
        e = mine_ref[at]
        for ref, scale in zip(coded_refs, scales):
            e = e + unpack(ref, rows, i).astype(jnp.float32) * scale
        sq = e * e
        sq_ref[at] = sq
        total = total + jnp.sum(sq, axis=0, keepdims=True)
    sum_ref[...] = total


def places(lists):
    place = lax.broadcasted_iota(jnp.int32, lists.shape, 1)
    bits = (place ^ 8) << ((lists & 7) * 4)
    none = sum(8 << (4 * i) for i in range(8)) - (1 << 32)
    words = [
        jnp.sum(jnp.where(lists >> 3 == h, bits, 0), axis=1, keepdims=True) ^ none
        for h in range(IB // 8)
    ]
    return [[word[k, 0] for word in words] for k in range(lists.shape[0])]


def product_kernel(masks, n_layer, n_row, n_col, lists_ref, *refs):
    n_slots, n_held = n_layer // 2, 2 * len(masks)
    mine_refs, near_refs = refs[:2], refs[2 : 2 + 2 * n_row]
    a_refs, out_refs = refs[2 + 2 * n_row : 2 + 2 * n_row + n_held], refs[2 + 2 * n_row + n_held : -1]
    lhs_ref = refs[-1]
    layer, row, col = (lax.axis_index(n) for n in ("layer", "row", "col"))
    per, per_row = IB // n_layer, n_col // n_row
    capacity, block, depth = a_refs[0].shape
    lists = places(lists_ref[...])
    rhs = []
    for k in range(n_held):
        other, place = k % 2, k // 2
        panel = col ^ masks[place]
        at = panel % per_row * depth
        owner = (panel // per_row) ^ row
        start = pl.multiple_of(owner * (per_row * depth) + at, depth)
        mine = mine_refs[other][pl.ds(start, depth), :]
        at = pl.ds(pl.multiple_of(at, depth), depth)
        near = near_refs[other][at, :]
        for i in range(1, n_row):
            near = jnp.where(owner == i, near_refs[2 * i + other][at, :], near)
        rhs.append(jnp.concatenate([mine, near], axis=1))
    rhs = jnp.concatenate(rhs, axis=0)
    width, parts = rhs.shape[1] // 2, []
    for slot in range(n_slots):
        for sub in range(per):
            block_row = (layer ^ (2 * slot)) * per + sub
            for k in range(n_held):
                word = lists[k][0]
                for h in range(1, len(lists[k])):
                    word = jnp.where(block_row // 8 == h, lists[k][h], word)
                n = (word >> (block_row % 8 * 4)) & 15
                a = a_refs[k][jnp.minimum(n, capacity - 1)]
                lhs_ref[slot, sub * block : (sub + 1) * block, k * depth : (k + 1) * depth] = (
                    jnp.where(n < capacity, a, jnp.zeros_like(a))
                )
        out = jnp.dot(lhs_ref[slot], rhs, preferred_element_type=jnp.float32)
        parts += [out[:, m * width : (m + 1) * width] for m in range(2)]
    out_refs[0][...] = parts[0]
    for k in range(1, 2 * n_slots - 1, 2):
        one, two = parts[k : k + 2]
        parts[k] = jnp.where(layer % 2 == 0, one, two)
        parts[k + 1] = jnp.where(layer % 2 == 0, two, one)
    pack(parts[1:], out_refs[1:])


def products(masks, lists, b_refs, panels):
    n_layer, n_row, n_col = (lax.axis_size(a) for a in ("layer", "row", "col"))
    _, block, depth = panels[0].shape
    rows, n_slots, width = IB // n_layer * block, n_layer // 2, b_refs[0].shape[1]
    ins = [lists, *b_refs, *panels]
    return pl.pallas_call(
        functools.partial(product_kernel, masks, n_layer, n_row, n_col),
        out_shape=[pltpu.VMEM((rows, width), jnp.float32)]
        + [pltpu.VMEM((rows // VALUES * WORDS + 8, width), jnp.int32)] * (2 * n_slots - 1),
        in_specs=[VMEM] * len(ins),
        out_specs=[VMEM] * (2 * n_slots),
        scratch_shapes=[
            pltpu.VMEM((n_slots, rows, len(panels) * depth), jnp.bfloat16),
        ],
        name="partial_rows",
    )(*(pin(x) for x in ins))


def body(a_blocks, a_rows, a_count, b_panel):
    n_layer, n_row, n_col = (lax.axis_size(a) for a in ("layer", "row", "col"))
    _, capacity, block, _ = a_blocks.shape

    def other(x):
        return xor_permute(x, "layer", 1)

    masks, panels = [0], [a_blocks[0]]
    valid = jnp.arange(capacity, dtype=jnp.int32)[None, :] < a_count[:, None]
    lists = jnp.where(valid, a_rows, IB)
    lists = jnp.concatenate([lists, other(lists)])
    bit = n_col // 2
    while bit > 1:
        panels = panels + [xor_permute(p, "col", bit) for p in panels]
        lists = jnp.concatenate([lists, xor_permute(lists, "col", bit)])
        masks = masks + [m ^ bit for m in masks]
        bit //= 2

    own_other = other(panels[0])
    b_panel, own_other = lax.optimization_barrier((b_panel, own_other))

    b_rows = [[b_panel, xor_permute(b_panel, "col", 1)]]
    bit = 1
    while bit < n_row:
        b_rows = b_rows + [[xor_permute(b, "row", bit) for b in pair] for pair in b_rows]
        bit *= 2

    mine = jnp.concatenate([pair[0] for pair in b_rows])
    mine = [mine, other(mine)]
    near = [pair[1] for pair in b_rows]
    own = a_blocks[0]
    first_other = other(near[0])
    far, lists, mine, near, own_other, first_other = lax.optimization_barrier(
        (panels[1:], lists, mine, near, own_other, first_other)
    )
    near = [near[0], first_other] + [x for b in near[1:] for x in (b, other(b))]
    panels = [own, own_other] + [x for p in far for x in (p, other(p))]
    b_refs = mine + near
    parts = products(masks, lists, b_refs, panels)

    masks = [(2 * (k // 2), 0, k % 2) for k in range(n_layer)]
    swaps = [0] + [k + 1 if k % 2 else k - 1 for k in range(1, n_layer - 1)] + [n_layer - 1]
    parts = [parts[0]] + [
        grid_permute(parts[k], masks[k], masks[swaps[k]]) for k in range(1, n_layer)
    ]
    sq, col_sum = pl.pallas_call(
        square_kernel,
        out_shape=(
            pltpu.VMEM(parts[0].shape, jnp.float32),
            pltpu.VMEM((1, parts[0].shape[1]), jnp.float32),
        ),
        in_specs=[VMEM] * len(parts),
        out_specs=(VMEM, VMEM),
        name="squares",
    )(*(pin(x) for x in parts))

    col_sum = sum_over_devices(col_sum)
    scale = 1.0 / (col_sum * (1.0 / (n_row * IB * block)) + 1e-06)
    return (sq * scale)[None]


def solution(mesh):
    return jax.shard_map(
        body,
        mesh=mesh,
        in_specs=(
            P(("layer", "row", "col"), None, None, None),
            P(("layer", "row", "col"), None),
            P(("layer", "row", "col")),
            P(("layer", "row"), "col"),
        ),
        out_specs=P("row", "layer", "col"),
        check_vma=False,
    )
```
